32 devices in a mesh: seq: 8 (over z, x), head: 4 (over y, core).
Axes of the slice: x: 2, y: 2, z: 4, core: 2. Of those that a mesh axis runs over, the one named last changes fastest.
Arguments:
- queries: bfloat16 [8192, 4096], P('seq', 'head'), may hold values from -0.23925781 to 0.23925781
- keys: bfloat16 [8192, 4096], P('seq', 'head'), may hold values from -0.23925781 to 0.23925781
- values: bfloat16 [8192, 4096], P('seq', 'head'), may hold values from -1.5 to 1.5
- out_grad: bfloat16 [8192, 4096], P('seq', 'head'), may hold values from -1.5 to 1.5
- starts: int32 [8192], P('seq'), may hold values 0 or 1
- owners: int32 [8192, 1], P('seq'), may hold values from 0 to 3; in each aligned block of 1024 rows (0 to 1023, 1024 to 2047, ...) at most 512 rows name the same one
Outputs:
- returned: bfloat16 [16384, 3, 4096], P(('seq', 'head'))
The draws below stay inside these ranges and needn't reach their ends.
Inputs may be any that keep to these rules, and one draw needn't show every extreme that they name: `owners`: among the 1024 tokens of one block, no owner is named by more than 512 tokens, a bound that some block reaches.
All inputs are finite; a program needn't handle non-finite values. No bound on the sum of `starts` on one device may be relied on, other than what follows from the above.
Results may differ from the reference program's by a relative error of at most 0.0049.
Values may be sent and summed in bfloat16 or wider, within the bound.
A program may use at most 128 MiB of HBM per device.

```python
import math
import jax
import jax.numpy as jnp
import numpy as np
from jax import lax

HD = 128
H = 32
SPAN = 1024
TOKENS = 8192
CAP = 512
N_SEQ = 8
N_HEAD = 4


def plant(array, key, smallest, top_value):
    extent = array.shape
    place = [jax.random.randint(jax.random.fold_in(key, axis), (), 0, extent[axis]) for axis in range(len(extent))]
    array = array.at[tuple(place)].set(smallest)
    longest = extent.index(max(extent))
    place[longest] = (place[longest] + 1) % extent[longest]
    return array.at[tuple(place)].set(top_value)


def level_of(rng, shape, pieces, low, largest):
    factor_of, own = 1.0, jax.random.fold_in(rng, 6)
    for dim, blocks in pieces:
        steps = jnp.exp(jax.random.uniform(jax.random.fold_in(own, dim), (blocks,), jnp.float32, low / len(pieces), largest / len(pieces)))
        factor_of = factor_of * jnp.repeat(steps, shape[dim] // blocks).reshape([-1 if axis == dim else 1 for axis in range(len(shape))])
    return factor_of


def shared_out(own_key, own, number, rows, amount, top, bound, slope):
    order = jax.random.permutation(own_key, amount)
    packed, common = shares(amount, rows * top, bound, slope, True), shares(amount, rows * top, bound, slope, False)
    places = jnp.arange(amount)

    def named(lengths, turn):
        used = int((lengths > 0).sum())
        fixed = max(1, used // 4)
        shifted = fixed + (places - fixed + turn * (used - fixed)) % max(1, amount - fixed)
        return jnp.zeros((amount,), jnp.int32).at[order[jnp.where(places < fixed, places, shifted)]].set(jnp.asarray(lengths, jnp.int32))

    lengths = jnp.where(number % 4 == 0, named(packed, number // 4), named(common, number - number // 4 - 1))
    mixed = jax.random.permutation(jax.random.fold_in(own, 3), amount)
    donor, sink = mixed[0:amount // 2 * 2:2], mixed[1:amount // 2 * 2:2]
    room = jnp.minimum(lengths[donor] - 1, bound - lengths[sink]) // 2
    room = jnp.where((donor == order[0]) | (sink == order[0]) | (lengths[sink] == 0), 0, jnp.maximum(room, 0))
    shifted = jax.random.randint(jax.random.fold_in(own, 4), (amount // 2,), 0, 1 << 20) % (room + 1)
    lengths = lengths.at[donor].add(-shifted).at[sink].add(shifted)
    members = jnp.searchsorted(jnp.cumsum(lengths), jnp.arange(rows * top), side="right").astype(jnp.int32)
    grid = members.reshape(top, rows).T
    grid = grid[jax.random.permutation(jax.random.fold_in(own, 1), rows)]
    turn = jax.random.randint(jax.random.fold_in(own, 2), (rows, 1), 0, top)
    return jnp.take_along_axis(grid, (jnp.arange(top)[None, :] + turn) % top, axis=1)


def shares(number_of, total, limit, slope, full):
    portions = [(1 << 20) // math.isqrt(rank ** slope) + 1 for rank in range(1, number_of + 1)]
    largest = limit if full else min(limit, max(-(-total // number_of), total * portions[0] // sum(portions)))
    least = 1 if total - largest >= number_of - 1 else 0
    given, rest = [largest] + [least] * (number_of - 1), total - largest - least * (number_of - 1)
    while rest > 0:
        free = [i for i in range(1, number_of) if given[i] < largest] or [i for i in range(1, number_of) if given[i] < limit]
        whole, budget = sum([portions[i] for i in free]), rest
        for i in free:
            more = min(limit - given[i], max(1, budget * portions[i] // whole), rest)
            given[i] = given[i] + more
            rest = rest - more
    return np.array(given)


def bell_draw(rng, extent, scale, reach, pieces=(), kind=jnp.bfloat16):
    drawn = scale * jax.random.normal(rng, extent, jnp.float32)
    if pieces:
        drawn = drawn * level_of(rng, extent, pieces, -0.22, 0.18)
    return jnp.clip(drawn, -reach, reach).astype(kind)


def setup_inputs(seed: int = 0) -> dict:
    arg_keys = jax.random.split(jax.random.key(seed), 7)
    queries = bell_draw(arg_keys[0], (TOKENS, H * HD), 0.04, 0.23925781, ((0, 8), (1, 4)))
    keys = bell_draw(arg_keys[1], (TOKENS, H * HD), 0.04, 0.23925781, ((0, 8), (1, 4)))
    values = bell_draw(arg_keys[2], (TOKENS, H * HD), 0.25, 1.5, ((0, 8), (1, 4)))
    out_grad = bell_draw(arg_keys[3], (TOKENS, H * HD), 0.25, 1.5, ((0, 8), (1, 4)))
    starts = plant((jax.random.randint(arg_keys[4], (TOKENS,), 0, 4 * SPAN) < 1).astype(jnp.int32), jax.random.fold_in(arg_keys[4], 1), 0, 1)
    owners_keys = jax.random.split(jax.random.fold_in(arg_keys[5], 1), TOKENS // SPAN)
    owners_turns = jax.random.permutation(jax.random.fold_in(arg_keys[5], 3), TOKENS // SPAN)
    owners = jax.vmap(lambda own, number: shared_out(jax.random.fold_in(arg_keys[5], 2), own, number, SPAN, N_HEAD, 1, CAP, 2))(owners_keys, owners_turns).reshape((TOKENS, 1))
    return {"queries": queries, "keys": keys, "values": values, "out_grad": out_grad, "starts": starts, "owners": owners}


def block_states(item):
    queries, keys, values, out_grad, starts = item
    segment = jnp.cumsum(starts, dtype=jnp.int32)
    first = (segment == 0).astype(jnp.bfloat16)[:, None, None]
    last = (segment == segment[-1]).astype(jnp.bfloat16)[:, None, None]
    keep = (segment[-1] == 0).astype(jnp.float32)
    query_h = queries.reshape(SPAN, H, HD).astype(jnp.float32)
    key_h = keys.reshape(SPAN, H, HD).astype(jnp.float32)
    value_h = values.reshape(SPAN, H, HD).astype(jnp.float32)
    grad_h = out_grad.reshape(SPAN, H, HD).astype(jnp.float32)
    fwd_local = jnp.einsum("thd,the->hde", key_h * last.astype(jnp.float32), value_h)
    bwd_local = jnp.einsum("thd,the->hde", query_h * first.astype(jnp.float32), grad_h)
    return keep, fwd_local, bwd_local


def block_grads(item):
    queries, keys, values, out_grad, starts, fwd_in, bwd_in = item
    segment = jnp.cumsum(starts, dtype=jnp.int32)
    position = jnp.arange(SPAN, dtype=jnp.int32)
    allowed = (position[None, :] <= position[:, None]) & (segment[:, None] == segment[None, :])
    first = (segment == 0).astype(jnp.float32)[:, None, None]
    last = (segment == segment[-1]).astype(jnp.float32)[:, None, None]
    query_h = queries.reshape(SPAN, H, HD).astype(jnp.float32)
    key_h = keys.reshape(SPAN, H, HD).astype(jnp.float32)
    value_h = values.reshape(SPAN, H, HD).astype(jnp.float32)
    grad_h = out_grad.reshape(SPAN, H, HD).astype(jnp.float32)
    score_ov = jnp.where(allowed[None], jnp.einsum("thd,shd->hts", grad_h, value_h), 0.0).astype(jnp.bfloat16).astype(jnp.float32)
    score_qk = jnp.where(allowed[None], jnp.einsum("thd,shd->hts", query_h, key_h), 0.0).astype(jnp.bfloat16).astype(jnp.float32)
    fwd_b = fwd_in.astype(jnp.bfloat16).astype(jnp.float32)
    bwd_b = bwd_in.astype(jnp.bfloat16).astype(jnp.float32)
    grad_q = jnp.einsum("hts,shd->thd", score_ov, key_h) + first * jnp.einsum("the,hde->thd", grad_h, fwd_b)
    grad_k = jnp.einsum("hts,thd->shd", score_ov, query_h) + last * jnp.einsum("the,hde->thd", value_h, bwd_b)
    grad_v = jnp.einsum("hts,thd->shd", score_qk, grad_h) + last * jnp.einsum("thd,hde->the", key_h, bwd_b)
    width = H * HD
    return (grad_q.reshape(SPAN, width).astype(jnp.bfloat16), grad_k.reshape(SPAN, width).astype(jnp.bfloat16), grad_v.reshape(SPAN, width).astype(jnp.bfloat16))


def chain_step(carry, item):
    keep, state = item
    return state + keep * carry, carry


def reference(queries, keys, values, out_grad, starts, owners):
    width = H * HD
    blocks = (queries.reshape(N_SEQ, SPAN, width), keys.reshape(N_SEQ, SPAN, width), values.reshape(N_SEQ, SPAN, width), out_grad.reshape(N_SEQ, SPAN, width), starts.reshape(N_SEQ, SPAN))
    keep, fwd_local, bwd_local = lax.map(block_states, blocks)
    zeros = jnp.zeros((H, HD, HD), jnp.float32)
    unused, fwd_in = lax.scan(chain_step, zeros, (keep, fwd_local))
    unused, bwd_in = lax.scan(chain_step, zeros, (keep, bwd_local), reverse=True)
    grad_q, grad_k, grad_v = lax.map(block_grads, blocks + (fwd_in, bwd_in))
    stacked = jnp.stack([grad_q.reshape(TOKENS, width), grad_k.reshape(TOKENS, width), grad_v.reshape(TOKENS, width)], axis=1)
    owner_ids = owners[:, 0].reshape(N_SEQ, SPAN).astype(jnp.int32)
    onehot = (owner_ids[:, :, None] == jnp.arange(N_HEAD, dtype=jnp.int32)[None, None, :]).astype(jnp.int32)
    before = jnp.cumsum(onehot, axis=1, dtype=jnp.int32) - onehot
    slots = jnp.sum(before * onehot, axis=2).astype(jnp.int32)
    block_index = jnp.arange(N_SEQ, dtype=jnp.int32)[:, None]
    target = ((block_index * N_HEAD + owner_ids) * CAP + slots).reshape(TOKENS).astype(jnp.int32)
    returned = jnp.zeros((N_SEQ * N_HEAD * CAP, 3, width), jnp.bfloat16).at[target].set(stacked)
    return returned
```

```python
import functools

import jax
import jax.numpy as jnp
from jax import lax
from jax.experimental import pallas as pl
from jax.experimental.pallas import tpu as pltpu
from jax.sharding import PartitionSpec as P

HD = 128
TILE = 256
KEEP_ROWS = 16
MESH = pl.DeviceIdType.MESH
F32 = jnp.float32
BF16 = jnp.bfloat16


def dot_nt(a, b):
    return lax.dot_general(a, b, (((1,), (1,)), ((), ())), preferred_element_type=F32)


def dot_tn(a, b):
    return lax.dot_general(a, b, (((0,), (0,)), ((), ())), preferred_element_type=F32)


def dot_nn(a, b):
    return jnp.dot(a, b, preferred_element_type=F32)


def kernel(
    n_seq,
    n_head,
    q_ref,
    k_ref,
    v_ref,
    o_ref,
    starts_ref,
    owners_ref,
    out_ref,
    mask,
    perm,
    first,
    last,
    tot_f,
    tot_b,
    in_f,
    in_b,
    keeps,
    snd,
    rcv,
    grads,
    acc_k,
    acc_v,
    send,
    st_send,
    st_recv,
    out_send,
    out_recv,
    own_sem,
):
    span, feats = q_ref.shape
    heads = feats // HD
    cap = 2 * span // n_head
    steps = n_seq.bit_length() - 1
    me_s = lax.axis_index("seq")
    me_h = lax.axis_index("head")

    def upper(step):
        return lax.rem(lax.div(me_s, 1 << step), 2)

    def partner(step):
        return me_s + (1 << step) * (1 - 2 * upper(step))

    barrier = pltpu.get_barrier_semaphore()
    for step in range(steps):
        pl.semaphore_signal(
            barrier, inc=1, device_id=(partner(step), me_h), device_id_type=MESH
        )
    for off in range(1, n_head):
        pl.semaphore_signal(
            barrier, inc=1, device_id=(me_s, lax.rem(me_h + off, n_head)), device_id_type=MESH
        )

    rows = 16
    row_id = lax.broadcasted_iota(jnp.int32, (rows, span), 0)
    owner = jnp.broadcast_to(owners_ref[...], (rows, span))
    start = jnp.broadcast_to(starts_ref[...], (rows, span)).astype(F32)
    onehot = jnp.where(row_id - 1 == owner, 1.0, 0.0)
    marks = jnp.where(row_id == 0, start, onehot)
    earlier = lax.broadcasted_iota(jnp.int32, (span, span), 0) <= lax.broadcasted_iota(
        jnp.int32, (span, span), 1
    )
    sums = dot_nn(marks.astype(BF16), jnp.where(earlier, 1.0, 0.0).astype(BF16))
    segment = sums[0:1, :]
    slot = jnp.sum(sums * onehot, axis=0, keepdims=True) - 1.0
    target = owners_ref[...] * cap + slot.astype(jnp.int32)
    wide = jnp.broadcast_to(segment, (HD, span)).T
    final = wide[span - 1 : span, :]
    first[...] = jnp.where(wide == 0.0, 1.0, 0.0)
    last[...] = jnp.where(wide == final, 1.0, 0.0)
    keep = jnp.broadcast_to(jnp.where(final == 0.0, 1.0, 0.0), (KEEP_ROWS, HD))
    for tile in range(span // TILE):
        base = tile * TILE
        same = wide[base : base + TILE, 0:1] == segment
        t_id = base + lax.broadcasted_iota(jnp.int32, (TILE, span), 0)
        s_id = lax.broadcasted_iota(jnp.int32, (TILE, span), 1)
        mask[base : base + TILE, :] = jnp.where(same & (s_id <= t_id), 1.0, 0.0)

    def fill(chunk, carry):
        base = pl.multiple_of(chunk * TILE, TILE)
        place = base + lax.broadcasted_iota(jnp.int32, (TILE, span), 0)
        perm[pl.ds(base, TILE), :] = jnp.where(place == target, 1.0, 0.0).astype(BF16)
        return carry

    def state_copy(step, h):
        return pltpu.make_async_remote_copy(
            src_ref=snd.at[step, h],
            dst_ref=rcv.at[step, h],
            send_sem=st_send.at[step, h],
            recv_sem=st_recv.at[step, h],
            device_id=(partner(step), me_h),
            device_id_type=MESH,
        )

    def state_send(step, h):
        snd[step, h, 0:HD, :] = tot_f[h].astype(BF16)
        snd[step, h, HD : 2 * HD, :] = tot_b[h].astype(BF16)
        snd[step, h, 2 * HD :, :] = keeps[h, 0].astype(BF16)
        state_copy(step, h).start()

    def columns(h):
        return pl.ds(pl.multiple_of(h * HD, HD), HD)

    def local_states(h):
        cols = columns(h)
        k_last = (k_ref[:, cols].astype(F32) * last[...]).astype(BF16)
        q_first = (q_ref[:, cols].astype(F32) * first[...]).astype(BF16)
        tot_f[h] = dot_tn(k_last, v_ref[:, cols])
        tot_b[h] = dot_tn(q_first, o_ref[:, cols])
        in_f[h] = jnp.zeros((HD, HD), F32)
        in_b[h] = jnp.zeros((HD, HD), F32)
        keeps[h, 0] = keep
        keeps[h, 1] = jnp.ones((KEEP_ROWS, HD), F32)
        keeps[h, 2] = jnp.ones((KEEP_ROWS, HD), F32)
        state_send(0, h)

    def combine(step, h):
        state_copy(step, h).wait_recv()
        up = jnp.broadcast_to(upper(step), (HD, HD)) == 1
        up_row = up[0:KEEP_ROWS, :]
        got_f = rcv[step, h, 0:HD, :].astype(F32)
        got_b = rcv[step, h, HD : 2 * HD, :].astype(F32)
        got_keep = rcv[step, h, 2 * HD :, :].astype(F32)
        whole, before, after = keeps[h, 0], keeps[h, 1], keeps[h, 2]
        in_f[h] = in_f[h] + jnp.where(up, before[0:1, :] * got_f, 0.0)
        in_b[h] = in_b[h] + jnp.where(up, 0.0, after[0:1, :] * got_b)
        keeps[h, 1] = jnp.where(up_row, before * got_keep, before)
        keeps[h, 2] = jnp.where(up_row, after, after * got_keep)
        if step < steps - 1:
            mine_f, mine_b = tot_f[h], tot_b[h]
            own, other = whole[0:1, :], got_keep[0:1, :]
            tot_f[h] = jnp.where(up, mine_f + own * got_f, got_f + other * mine_f)
            tot_b[h] = jnp.where(up, got_b + other * mine_b, mine_b + own * got_b)
            keeps[h, 0] = whole * got_keep
            state_send(step + 1, h)

    def out_columns(source, h):
        return pl.ds(pl.multiple_of((source * heads + h) * HD, HD), HD)

    def out_copy(off, h):
        peer = lax.rem(me_h + off, n_head)
        return pltpu.make_async_remote_copy(
            src_ref=send.at[h, off],
            dst_ref=out_ref.at[:, :, out_columns(me_h, h)],
            send_sem=out_send.at[h, off],
            recv_sem=out_recv.at[h, off],
            device_id=(me_s, peer),
            device_id_type=MESH,
        )

    def own_copy(h):
        return pltpu.make_async_copy(
            send.at[h, 0], out_ref.at[:, :, out_columns(me_h, h)], own_sem.at[h]
        )

    far_first = [n_head // 2] + [o for o in range(1, n_head) if o != n_head // 2] + [0]

    def gradients(h):
        cols = columns(h)
        fwd = in_f[h].astype(BF16)
        bwd = in_b[h].astype(BF16)
        for tile in reversed(range(span // TILE)):
            here = slice(tile * TILE, (tile + 1) * TILE)
            width = (tile + 1) * TILE
            allowed = mask[here, 0:width]
            o_t = o_ref[here, cols]
            q_t = q_ref[here, cols]
            k_s = k_ref[0:width, cols]
            weight = (dot_nt(o_t, v_ref[0:width, cols]) * allowed).astype(BF16)
            grad_q = dot_nn(weight, k_s) + first[here, :] * dot_nt(o_t, fwd)
            grads[here, 0:HD] = grad_q.astype(BF16)
            add_k = dot_tn(weight, q_t)
            weight = (dot_nt(q_t, k_s) * allowed).astype(BF16)
            add_v = dot_tn(weight, o_t)
            if width == span:
                acc_k[...] = add_k
                acc_v[...] = add_v
            else:
                acc_k[0:width, :] += add_k
                acc_v[0:width, :] += add_v
        grad_k = acc_k[...] + last[...] * dot_nt(v_ref[:, cols], bwd)
        grad_v = acc_v[...] + last[...] * dot_nn(k_ref[:, cols], bwd)
        grads[:, HD : 2 * HD] = grad_k.astype(BF16)
        grads[:, 2 * HD :] = grad_v.astype(BF16)
        for off in far_first:
            base = pl.multiple_of(lax.rem(me_h + off, n_head) * cap, cap)
            placed = dot_nn(perm[pl.ds(base, cap), :], grads[...]).astype(BF16)
            for part in range(3):
                send[h, off, part] = placed[:, part * HD : (part + 1) * HD]
            if off == 0:
                own_copy(h).start()
            else:
                out_copy(off, h).start()

    pl.semaphore_wait(barrier, steps + n_head - 1)

    def turn(t, carry):
        for lag in range(steps, -1, -1):
            h = t - lag

            @pl.when((h >= 0) & (h < heads))
            def _():
                if lag == 0:
                    local_states(h)
                else:
                    combine(lag - 1, h)

        @pl.when(t == 1)
        def _():
            lax.fori_loop(0, n_head * cap // TILE, fill, 0)

        @pl.when((t >= steps) & (t - steps < heads))
        def _():
            gradients(t - steps)

        return carry

    lax.fori_loop(0, heads + steps, turn, 0)

    def finish(h, carry):
        for step in range(steps):
            state_copy(step, h).wait_send()
        for off in range(1, n_head):
            out_copy(off, h).wait_send()
            source = lax.rem(me_h + n_head - off, n_head)
            pltpu.make_async_remote_copy(
                src_ref=send.at[h, off],
                dst_ref=out_ref.at[:, :, out_columns(source, h)],
                send_sem=out_send.at[h, off],
                recv_sem=out_recv.at[h, off],
                device_id=(me_s, source),
                device_id_type=MESH,
            ).wait_recv()
        own_copy(h).wait()
        return carry

    lax.fori_loop(0, heads, finish, 0)


def shards(n_seq, n_head, queries, keys, values, out_grad, starts, owners):
    span, feats = queries.shape
    heads = feats // HD
    cap = 2 * span // n_head
    steps = n_seq.bit_length() - 1
    vmem = pl.BlockSpec(memory_space=pltpu.VMEM)
    flops = heads * (10 * span * span * HD + 12 * span * span * HD)
    out = pl.pallas_call(
        functools.partial(kernel, n_seq, n_head),
        out_shape=jax.ShapeDtypeStruct((3, cap, n_head * feats), BF16),
        in_specs=[vmem] * 6,
        out_specs=pl.BlockSpec(memory_space=pl.ANY),
        scratch_shapes=[
            pltpu.VMEM((span, span), F32),
            pltpu.VMEM((n_head * cap, span), BF16),
            pltpu.VMEM((span, HD), F32),
            pltpu.VMEM((span, HD), F32),
            pltpu.VMEM((heads, HD, HD), F32),
            pltpu.VMEM((heads, HD, HD), F32),
            pltpu.VMEM((heads, HD, HD), F32),
            pltpu.VMEM((heads, HD, HD), F32),
            pltpu.VMEM((heads, 3, KEEP_ROWS, HD), F32),
            pltpu.VMEM((steps, heads, 2 * HD + KEEP_ROWS, HD), BF16),
            pltpu.VMEM((steps, heads, 2 * HD + KEEP_ROWS, HD), BF16),
            pltpu.VMEM((span, 3 * HD), BF16),
            pltpu.VMEM((span, HD), F32),
            pltpu.VMEM((span, HD), F32),
            pltpu.VMEM((heads, n_head, 3, cap, HD), BF16),
            pltpu.SemaphoreType.DMA((steps, heads)),
            pltpu.SemaphoreType.DMA((steps, heads)),
            pltpu.SemaphoreType.DMA((heads, n_head)),
            pltpu.SemaphoreType.DMA((heads, n_head)),
            pltpu.SemaphoreType.DMA((heads,)),
        ],
        compiler_params=pltpu.CompilerParams(
            collective_id=0, has_side_effects=True, vmem_limit_bytes=56 * 1024 * 1024
        ),
        cost_estimate=pl.CostEstimate(
            flops=flops, bytes_accessed=22 * span * feats, transcendentals=0
        ),
    )(queries, keys, values, out_grad, starts.reshape(1, span), owners.reshape(1, span))
    return out.transpose(1, 0, 2)


def solution(mesh):
    in_specs = (
        P("seq", "head"),
        P("seq", "head"),
        P("seq", "head"),
        P("seq", "head"),
        P("seq"),
        P("seq", None),
    )
    return jax.shard_map(
        functools.partial(shards, mesh.shape["seq"], mesh.shape["head"]),
        mesh=mesh,
        in_specs=in_specs,
        out_specs=P(("seq", "head"), None, None),
        check_vma=False,
    )
```

```python
import functools

import jax
import jax.numpy as jnp
from jax import lax
from jax.experimental import pallas as pl
from jax.experimental.pallas import tpu as pltpu
from jax.sharding import PartitionSpec as P

HD = 128
TILE = 256
KEEP_ROWS = 16
LIST_SHARE = (13, 16)
MESH = pl.DeviceIdType.MESH
F32 = jnp.float32
BF16 = jnp.bfloat16


def list_rows(cap):
    return 2 * cap * LIST_SHARE[0] // LIST_SHARE[1] // 16 * 16


def dot_nt(a, b):
    return lax.dot_general(a, b, (((1,), (1,)), ((), ())), preferred_element_type=F32)


def dot_tn(a, b):
    return lax.dot_general(a, b, (((0,), (0,)), ((), ())), preferred_element_type=F32)


def dot_nn(a, b):
    return jnp.dot(a, b, preferred_element_type=F32)


def kernel(
    n_seq,
    n_head,
    q_ref,
    k_ref,
    v_ref,
    o_ref,
    starts_ref,
    owners_ref,
    near_ref,
    far_ref,
    rest_ref,
    info_ref,
    mask,
    perm,
    first,
    last,
    tot_f,
    tot_b,
    in_f,
    in_b,
    keeps,
    snd,
    rcv,
    grads,
    acc_k,
    acc_v,
    over,
    counts,
    near_buf,
    far_buf,
    st_send,
    st_recv,
    near_send,
    near_recv,
    own_sem,
    far_send,
    far_recv,
    rest_sem,
    fwd_send,
    fwd_recv,
):
    span, feats = q_ref.shape
    heads = feats // HD
    cap = 2 * span // n_head
    steps = n_seq.bit_length() - 1
    me_s = lax.axis_index("seq")
    me_h = lax.axis_index("head")
    chips = n_head // 2
    my_chip, my_core = lax.div(me_h, 2), lax.rem(me_h, 2)
    sibling = me_h + 1 - 2 * my_core
    listed = list_rows(cap)

    def upper(step):
        return lax.rem(lax.div(me_s, 1 << step), 2)

    def partner(step):
        return me_s + (1 << step) * (1 - 2 * upper(step))

    def far_peer(co):
        return 2 * lax.rem(my_chip + co, chips) + my_core

    barrier = pltpu.get_barrier_semaphore()
    for step in range(steps):
        pl.semaphore_signal(
            barrier, inc=1, device_id=(partner(step), me_h), device_id_type=MESH
        )
    for peer in [sibling] + [far_peer(co) for co in range(1, chips)]:
        pl.semaphore_signal(barrier, inc=1, device_id=(me_s, peer), device_id_type=MESH)

    rows = 16
    row_id = lax.broadcasted_iota(jnp.int32, (rows, span), 0)
    owner = jnp.broadcast_to(owners_ref[...], (rows, span))
    start = jnp.broadcast_to(starts_ref[...], (rows, span)).astype(F32)
    onehot = jnp.where(row_id - 1 == owner, 1.0, 0.0)
    marks = jnp.where(row_id == 0, start, onehot)
    earlier = lax.broadcasted_iota(jnp.int32, (span, span), 0) <= lax.broadcasted_iota(
        jnp.int32, (span, span), 1
    )
    sums = dot_nn(marks.astype(BF16), jnp.where(earlier, 1.0, 0.0).astype(BF16))
    segment = sums[0:1, :]
    slot = jnp.sum(sums * onehot, axis=0, keepdims=True) - 1.0
    totals = jnp.broadcast_to(jnp.sum(marks, axis=1, keepdims=True), (rows, span))
    owner_chip = owner // 2
    evens = jnp.sum(jnp.where(row_id - 1 == 2 * owner_chip, totals, 0.0), axis=0, keepdims=True)
    own_row = owners_ref[...]
    chip_row = own_row // 2
    odd_row = own_row - 2 * chip_row
    lift = jnp.where(chip_row == my_chip, cap, evens.astype(jnp.int32))
    target = chip_row * (2 * cap) + odd_row * lift + slot.astype(jnp.int32)
    counts[...] = totals[:, 0:HD]
    full = jnp.zeros((1, HD), F32)
    for chip in range(chips):
        pair = counts[2 * chip + 1 : 2 * chip + 2, :] + counts[2 * chip + 2 : 2 * chip + 3, :]
        full = jnp.maximum(full, jnp.where(pair > listed, 1.0, 0.0))
    over[...] = jnp.broadcast_to(full, (KEEP_ROWS, HD))
    lane_row = lax.broadcasted_iota(jnp.int32, (rows, HD), 0)
    mine = jnp.sum(jnp.where(lane_row - 1 == me_h, counts[...], 0.0), axis=0, keepdims=True)
    even = jnp.where(lane_row - 1 == me_h - 1, counts[...], 0.0)
    shift = jnp.sum(even, axis=0, keepdims=True) * my_core.astype(F32)
    info_ref[8:16, :] = jnp.broadcast_to(shift, (8, HD))
    info_ref[16:24, :] = jnp.broadcast_to(mine, (8, HD))
    wide = jnp.broadcast_to(segment, (HD, span)).T
    final = wide[span - 1 : span, :]
    first[...] = jnp.where(wide == 0.0, 1.0, 0.0)
    last[...] = jnp.where(wide == final, 1.0, 0.0)
    keep = jnp.broadcast_to(jnp.where(final == 0.0, 1.0, 0.0), (KEEP_ROWS, HD))
    for tile in range(span // TILE):
        base = tile * TILE
        same = wide[base : base + TILE, 0:1] == segment
        t_id = base + lax.broadcasted_iota(jnp.int32, (TILE, span), 0)
        s_id = lax.broadcasted_iota(jnp.int32, (TILE, span), 1)
        mask[base : base + TILE, :] = jnp.where(same & (s_id <= t_id), 1.0, 0.0)

    def fill(chunk, carry):
        base = pl.multiple_of(chunk * TILE, TILE)
        place = base + lax.broadcasted_iota(jnp.int32, (TILE, span), 0)
        perm[pl.ds(base, TILE), :] = jnp.where(place == target, 1.0, 0.0).astype(BF16)
        return carry

    def state_copy(step, h):
        return pltpu.make_async_remote_copy(
            src_ref=snd.at[step, h],
            dst_ref=rcv.at[step, h],
            send_sem=st_send.at[step, h],
            recv_sem=st_recv.at[step, h],
            device_id=(partner(step), me_h),
            device_id_type=MESH,
        )

    def state_send(step, h):
        snd[step, h, 0:HD, :] = tot_f[h].astype(BF16)
        snd[step, h, HD : 2 * HD, :] = tot_b[h].astype(BF16)
        snd[step, h, 2 * HD : 2 * HD + KEEP_ROWS, :] = keeps[h, 0].astype(BF16)
        snd[step, h, 2 * HD + KEEP_ROWS :, :] = over[...].astype(BF16)
        state_copy(step, h).start()

    def columns(h):
        return pl.ds(pl.multiple_of(h * HD, HD), HD)

    def local_states(h):
        cols = columns(h)
        k_last = (k_ref[:, cols].astype(F32) * last[...]).astype(BF16)
        q_first = (q_ref[:, cols].astype(F32) * first[...]).astype(BF16)
        tot_f[h] = dot_tn(k_last, v_ref[:, cols])
        tot_b[h] = dot_tn(q_first, o_ref[:, cols])
        in_f[h] = jnp.zeros((HD, HD), F32)
        in_b[h] = jnp.zeros((HD, HD), F32)
        keeps[h, 0] = keep
        keeps[h, 1] = jnp.ones((KEEP_ROWS, HD), F32)
        keeps[h, 2] = jnp.ones((KEEP_ROWS, HD), F32)
        state_send(0, h)

    def combine(step, h):
        state_copy(step, h).wait_recv()
        up = jnp.broadcast_to(upper(step), (HD, HD)) == 1
        up_row = up[0:KEEP_ROWS, :]
        got_f = rcv[step, h, 0:HD, :].astype(F32)
        got_b = rcv[step, h, HD : 2 * HD, :].astype(F32)
        got_keep = rcv[step, h, 2 * HD : 2 * HD + KEEP_ROWS, :].astype(F32)
        over[...] = jnp.maximum(over[...], rcv[step, h, 2 * HD + KEEP_ROWS :, :].astype(F32))
        whole, before, after = keeps[h, 0], keeps[h, 1], keeps[h, 2]
        in_f[h] = in_f[h] + jnp.where(up, before[0:1, :] * got_f, 0.0)
        in_b[h] = in_b[h] + jnp.where(up, 0.0, after[0:1, :] * got_b)
        keeps[h, 1] = jnp.where(up_row, before * got_keep, before)
        keeps[h, 2] = jnp.where(up_row, after, after * got_keep)
        if step < steps - 1:
            mine_f, mine_b = tot_f[h], tot_b[h]
            own, other = whole[0:1, :], got_keep[0:1, :]
            tot_f[h] = jnp.where(up, mine_f + own * got_f, got_f + other * mine_f)
            tot_b[h] = jnp.where(up, got_b + other * mine_b, mine_b + own * got_b)
            keeps[h, 0] = whole * got_keep
            state_send(step + 1, h)

    def near_copy(h):
        return pltpu.make_async_remote_copy(
            src_ref=near_buf.at[h, 1],
            dst_ref=near_ref.at[my_core, :, :, columns(h)],
            send_sem=near_send.at[h],
            recv_sem=near_recv.at[h],
            device_id=(me_s, sibling),
            device_id_type=MESH,
        )

    def own_copy(h):
        return pltpu.make_async_copy(
            near_buf.at[h, 0], near_ref.at[my_core, :, :, columns(h)], own_sem.at[h]
        )

    def far_copy(co, h):
        return pltpu.make_async_remote_copy(
            src_ref=far_buf.at[h, co - 1, :, 0:listed],
            dst_ref=far_ref.at[co - 1, my_core, :, :, columns(h)],
            send_sem=far_send.at[h, co - 1],
            recv_sem=far_recv.at[h, co - 1],
            device_id=(me_s, far_peer(co)),
            device_id_type=MESH,
        )

    def rest_copy(co, h):
        return pltpu.make_async_copy(
            far_buf.at[h, co - 1, :, listed : 2 * cap],
            rest_ref.at[co - 1, :, :, columns(h)],
            rest_sem.at[h, co - 1],
        )

    def pass_on(co, h):
        return pltpu.make_async_remote_copy(
            src_ref=far_ref.at[co - 1, my_core, :, :, columns(h)],
            dst_ref=far_ref.at[co - 1, my_core, :, :, columns(h)],
            send_sem=fwd_send.at[h, co - 1],
            recv_sem=fwd_recv.at[h, co - 1],
            device_id=(me_s, sibling),
            device_id_type=MESH,
        )

    def gradients(h):
        cols = columns(h)
        fwd = in_f[h].astype(BF16)
        bwd = in_b[h].astype(BF16)
        for tile in reversed(range(span // TILE)):
            here = slice(tile * TILE, (tile + 1) * TILE)
            width = (tile + 1) * TILE
            allowed = mask[here, 0:width]
            o_t = o_ref[here, cols]
            q_t = q_ref[here, cols]
            k_s = k_ref[0:width, cols]
            weight = (dot_nt(o_t, v_ref[0:width, cols]) * allowed).astype(BF16)
            grad_q = dot_nn(weight, k_s) + first[here, :] * dot_nt(o_t, fwd)
            grads[here, 0:HD] = grad_q.astype(BF16)
            add_k = dot_tn(weight, q_t)
            weight = (dot_nt(q_t, k_s) * allowed).astype(BF16)
            add_v = dot_tn(weight, o_t)
            if width == span:
                acc_k[...] = add_k
                acc_v[...] = add_v
            else:
                acc_k[0:width, :] += add_k
                acc_v[0:width, :] += add_v
        grad_k = acc_k[...] + last[...] * dot_nt(v_ref[:, cols], bwd)
        grad_v = acc_v[...] + last[...] * dot_nn(k_ref[:, cols], bwd)
        grads[:, HD : 2 * HD] = grad_k.astype(BF16)
        grads[:, 2 * HD :] = grad_v.astype(BF16)
        for co in range(1, chips):
            base = pl.multiple_of(lax.rem(my_chip + co, chips) * (2 * cap), 2 * cap)
            for half in range(2):
                spot = pl.multiple_of(base + half * cap, cap)
                placed = dot_nn(perm[pl.ds(spot, cap), :], grads[...]).astype(BF16)
                for part in range(3):
                    far_buf[h, co - 1, part, half * cap : (half + 1) * cap] = placed[
                        :, part * HD : (part + 1) * HD
                    ]
            far_copy(co, h).start()
            rest_copy(co, h).start()
        for place, peer in ((1, sibling), (0, me_h)):
            base = pl.multiple_of(peer * cap, cap)
            placed = dot_nn(perm[pl.ds(base, cap), :], grads[...]).astype(BF16)
            for part in range(3):
                near_buf[h, place, part] = placed[:, part * HD : (part + 1) * HD]
        near_copy(h).start()
        own_copy(h).start()

    pl.semaphore_wait(barrier, steps + chips)

    def turn(t, carry):
        for lag in range(steps, -1, -1):
            h = t - lag

            @pl.when((h >= 0) & (h < heads))
            def _():
                if lag == 0:
                    local_states(h)
                else:
                    combine(lag - 1, h)

        @pl.when(t == 1)
        def _():
            lax.fori_loop(0, n_head * cap // TILE, fill, 0)

        @pl.when((t >= steps) & (t - steps < heads))
        def _():
            gradients(t - steps)

        return carry

    lax.fori_loop(0, heads + steps, turn, 0)

    info_ref[0:8, :] = over[0:8, :]

    def forward(h, carry):
        for co in range(1, chips):
            far_copy(co, h).wait_recv()
            pass_on(co, h).start()
        return carry

    lax.fori_loop(0, heads, forward, 0)

    def finish(h, carry):
        for step in range(steps):
            state_copy(step, h).wait_send()
        for co in range(1, chips):
            far_copy(co, h).wait_send()
            rest_copy(co, h).wait()
            pass_on(co, h).wait_send()
            pass_on(co, h).wait_recv()
        near_copy(h).wait_send()
        near_copy(h).wait_recv()
        own_copy(h).wait()
        return carry

    lax.fori_loop(0, heads, finish, 0)


def rest_kernel(n_head, mine_ref, rest_ref, far_send, far_recv, fwd_send, fwd_recv):
    chips = n_head // 2
    me_s = lax.axis_index("seq")
    me_h = lax.axis_index("head")
    my_chip, my_core = lax.div(me_h, 2), lax.rem(me_h, 2)
    sibling = me_h + 1 - 2 * my_core

    def far_peer(co):
        return 2 * lax.rem(my_chip + co, chips) + my_core

    def far_copy(co):
        return pltpu.make_async_remote_copy(
            src_ref=mine_ref.at[co - 1],
            dst_ref=rest_ref.at[co - 1, my_core],
            send_sem=far_send.at[co - 1],
            recv_sem=far_recv.at[co - 1],
            device_id=(me_s, far_peer(co)),
            device_id_type=MESH,
        )

    def pass_on(co):
        return pltpu.make_async_remote_copy(
            src_ref=rest_ref.at[co - 1, my_core],
            dst_ref=rest_ref.at[co - 1, my_core],
            send_sem=fwd_send.at[co - 1],
            recv_sem=fwd_recv.at[co - 1],
            device_id=(me_s, sibling),
            device_id_type=MESH,
        )

    barrier = pltpu.get_barrier_semaphore()
    for peer in [sibling] + [far_peer(co) for co in range(1, chips)]:
        pl.semaphore_signal(barrier, inc=1, device_id=(me_s, peer), device_id_type=MESH)
    pl.semaphore_wait(barrier, chips)
    for co in range(1, chips):
        far_copy(co).start()
    for co in range(1, chips):
        far_copy(co).wait_recv()
        pass_on(co).start()
    for co in range(1, chips):
        far_copy(co).wait_send()
        pass_on(co).wait_send()
        pass_on(co).wait_recv()


def rest_call(n_head, mine):
    lists, parts, rows, feats = mine.shape
    sems = pltpu.SemaphoreType.DMA((lists,))
    return pl.pallas_call(
        functools.partial(rest_kernel, n_head),
        out_shape=jax.ShapeDtypeStruct((lists, 2, parts, rows, feats), BF16),
        in_specs=[pl.BlockSpec(memory_space=pl.ANY)],
        out_specs=pl.BlockSpec(memory_space=pl.ANY),
        scratch_shapes=[sems] * 4,
        compiler_params=pltpu.CompilerParams(collective_id=1, has_side_effects=True),
    )(mine)


def place_kernel(chip_ref, info_ref, near_ref, *refs):
    *lists, out_ref, pick = refs
    cap = out_ref.shape[1]
    source = pl.program_id(1)

    @pl.when((pl.program_id(0) == 0) & (source == 0) & (pl.program_id(2) == 0))
    def _():
        slot = lax.broadcasted_iota(jnp.int32, pick.shape, 0)
        place = lax.broadcasted_iota(jnp.int32, pick.shape, 1)
        shift = info_ref[8:9, 0:1].astype(jnp.int32)
        count = info_ref[16:17, 0:1].astype(jnp.int32)
        pick[...] = jnp.where((place == slot + shift) & (slot < count), 1.0, 0.0).astype(BF16)

    @pl.when(source < 2)
    def _():
        out_ref[...] = near_ref[0]

    @pl.when(source >= 2)
    def _():
        base, total = 0, None
        for ref in lists:
            rows = ref.shape[3]
            term = dot_nn(pick[:, base : base + rows], ref[0, 0, 0])
            total = term if total is None else total + term
            base += rows
        out_ref[0] = total.astype(BF16)


def place_call(n_head, info, near, *lists):
    _, parts, cap, feats = near.shape
    chips = n_head // 2
    wide = 512
    blocks = feats // wide
    chip = lax.div(lax.axis_index("head"), 2).astype(jnp.int32).reshape(1)

    def near_map(part, source, block, chip_ref):
        here = source < 2
        return (
            jnp.where(here, source, 1),
            part,
            0,
            jnp.where(here, block, blocks - 1),
        )

    def list_map(part, source, block, chip_ref):
        there = source >= 2
        place = jnp.where(there, source - 2, 0)
        return (place // 2, place % 2, part, 0, jnp.where(there, block, 0))

    def out_map(part, source, block, chip_ref):
        origin = lax.rem(chip_ref[0] + chips - source // 2, chips) * 2 + source % 2
        return (part, 0, origin * blocks + block)

    return pl.pallas_call(
        place_kernel,
        out_shape=jax.ShapeDtypeStruct((parts, cap, n_head * feats), BF16),
        grid_spec=pltpu.PrefetchScalarGridSpec(
            num_scalar_prefetch=1,
            grid=(parts, n_head, blocks),
            in_specs=[
                pl.BlockSpec((24, HD), lambda part, source, block, chip_ref: (0, 0)),
                pl.BlockSpec((1, 1, cap, wide), near_map),
            ]
            + [pl.BlockSpec((1, 1, 1, a.shape[3], wide), list_map) for a in lists],
            out_specs=pl.BlockSpec((1, cap, wide), out_map),
            scratch_shapes=[pltpu.VMEM((cap, sum(a.shape[3] for a in lists)), BF16)],
        ),
        compiler_params=pltpu.CompilerParams(vmem_limit_bytes=58 * 1024 * 1024),
    )(chip, info, near, *lists)


def shards(n_seq, n_head, queries, keys, values, out_grad, starts, owners):
    span, feats = queries.shape
    heads = feats // HD
    cap = 2 * span // n_head
    steps = n_seq.bit_length() - 1
    vmem = pl.BlockSpec(memory_space=pltpu.VMEM)
    flops = heads * (10 * span * span * HD + 12 * span * span * HD)
    chips = n_head // 2
    listed = list_rows(cap)
    hbm = pl.BlockSpec(memory_space=pl.ANY)
    near, far, rest, info = pl.pallas_call(
        functools.partial(kernel, n_seq, n_head),
        out_shape=[
            jax.ShapeDtypeStruct((2, 3, cap, feats), BF16),
            jax.ShapeDtypeStruct((chips - 1, 2, 3, listed, feats), BF16),
            jax.ShapeDtypeStruct((chips - 1, 3, 2 * cap - listed, feats), BF16),
            jax.ShapeDtypeStruct((24, HD), F32),
        ],
        in_specs=[vmem] * 6,
        out_specs=[hbm, hbm, hbm, vmem],
        scratch_shapes=[
            pltpu.VMEM((span, span), F32),
            pltpu.VMEM((n_head * cap, span), BF16),
            pltpu.VMEM((span, HD), F32),
            pltpu.VMEM((span, HD), F32),
            pltpu.VMEM((heads, HD, HD), F32),
            pltpu.VMEM((heads, HD, HD), F32),
            pltpu.VMEM((heads, HD, HD), F32),
            pltpu.VMEM((heads, HD, HD), F32),
            pltpu.VMEM((heads, 3, KEEP_ROWS, HD), F32),
            pltpu.VMEM((steps, heads, 2 * HD + 2 * KEEP_ROWS, HD), BF16),
            pltpu.VMEM((steps, heads, 2 * HD + 2 * KEEP_ROWS, HD), BF16),
            pltpu.VMEM((span, 3 * HD), BF16),
            pltpu.VMEM((span, HD), F32),
            pltpu.VMEM((span, HD), F32),
            pltpu.VMEM((KEEP_ROWS, HD), F32),
            pltpu.VMEM((16, HD), F32),
            pltpu.VMEM((heads, 2, 3, cap, HD), BF16),
            pltpu.VMEM((heads, chips - 1, 3, 2 * cap, HD), BF16),
            pltpu.SemaphoreType.DMA((steps, heads)),
            pltpu.SemaphoreType.DMA((steps, heads)),
            pltpu.SemaphoreType.DMA((heads,)),
            pltpu.SemaphoreType.DMA((heads,)),
            pltpu.SemaphoreType.DMA((heads,)),
            pltpu.SemaphoreType.DMA((heads, chips - 1)),
            pltpu.SemaphoreType.DMA((heads, chips - 1)),
            pltpu.SemaphoreType.DMA((heads, chips - 1)),
            pltpu.SemaphoreType.DMA((heads, chips - 1)),
            pltpu.SemaphoreType.DMA((heads, chips - 1)),
        ],
        compiler_params=pltpu.CompilerParams(
            collective_id=0, has_side_effects=True, vmem_limit_bytes=56 * 1024 * 1024
        ),
        cost_estimate=pl.CostEstimate(
            flops=flops, bytes_accessed=22 * span * feats, transcendentals=0
        ),
    )(queries, keys, values, out_grad, starts.reshape(1, span), owners.reshape(1, span))
    out = lax.cond(
        info[0, 0] > 0.0,
        lambda: place_call(n_head, info, near, far, rest_call(n_head, rest)),
        lambda: place_call(n_head, info, near, far),
    )
    return out.transpose(1, 0, 2)


def solution(mesh):
    in_specs = (
        P("seq", "head"),
        P("seq", "head"),
        P("seq", "head"),
        P("seq", "head"),
        P("seq"),
        P("seq", None),
    )
    return jax.shard_map(
        functools.partial(shards, mesh.shape["seq"], mesh.shape["head"]),
        mesh=mesh,
        in_specs=in_specs,
        out_specs=P(("seq", "head"), None, None),
        check_vma=False,
    )
```

```python
import functools

import jax
import jax.numpy as jnp
from jax import lax
from jax.experimental import pallas as pl
from jax.experimental.pallas import tpu as pltpu
from jax.sharding import PartitionSpec as P

HD = 128
TILE = 256
KEEP_ROWS = 16
LIST_SHARE = (13, 16)
MESH = pl.DeviceIdType.MESH
F32 = jnp.float32
BF16 = jnp.bfloat16


def list_rows(cap):
    return 2 * cap * LIST_SHARE[0] // LIST_SHARE[1] // 16 * 16


def dot_nt(a, b):
    return lax.dot_general(a, b, (((1,), (1,)), ((), ())), preferred_element_type=F32)


def dot_tn(a, b):
    return lax.dot_general(a, b, (((0,), (0,)), ((), ())), preferred_element_type=F32)


def dot_nn(a, b):
    return jnp.dot(a, b, preferred_element_type=F32)


def kernel(
    n_seq,
    n_head,
    q_ref,
    k_ref,
    v_ref,
    o_ref,
    starts_ref,
    owners_ref,
    near_ref,
    far_ref,
    rest_ref,
    info_ref,
    mask,
    perm,
    first,
    last,
    tot_f,
    tot_b,
    in_f,
    in_b,
    keeps,
    snd,
    rcv,
    grads,
    acc_k,
    acc_v,
    over,
    counts,
    seg_col,
    seg_row,
    acc_q,
    near_buf,
    far_buf,
    st_send,
    st_recv,
    near_send,
    near_recv,
    own_sem,
    far_send,
    far_recv,
    rest_sem,
    fwd_send,
    fwd_recv,
):
    span, feats = q_ref.shape
    heads = feats // HD
    cap = 2 * span // n_head
    steps = n_seq.bit_length() - 1
    me_s = lax.axis_index("seq")
    me_h = lax.axis_index("head")
    chips = n_head // 2
    my_chip, my_core = lax.div(me_h, 2), lax.rem(me_h, 2)
    sibling = me_h + 1 - 2 * my_core
    listed = list_rows(cap)

    def upper(step):
        return lax.rem(lax.div(me_s, 1 << step), 2)

    def partner(step):
        return me_s + (1 << step) * (1 - 2 * upper(step))

    def far_peer(co):
        return 2 * lax.rem(my_chip + co, chips) + my_core

    barrier = pltpu.get_barrier_semaphore()
    for step in range(steps):
        pl.semaphore_signal(
            barrier, inc=1, device_id=(partner(step), me_h), device_id_type=MESH
        )
    for peer in [sibling] + [far_peer(co) for co in range(1, chips)]:
        pl.semaphore_signal(barrier, inc=1, device_id=(me_s, peer), device_id_type=MESH)

    rows = 16
    row_id = lax.broadcasted_iota(jnp.int32, (rows, span), 0)
    owner = jnp.broadcast_to(owners_ref[...], (rows, span))
    start = jnp.broadcast_to(starts_ref[...], (rows, span)).astype(F32)
    onehot = jnp.where(row_id - 1 == owner, 1.0, 0.0)
    marks = jnp.where(row_id == 0, start, onehot)
    earlier = lax.broadcasted_iota(jnp.int32, (span, span), 0) <= lax.broadcasted_iota(
        jnp.int32, (span, span), 1
    )
    sums = dot_nn(marks.astype(BF16), jnp.where(earlier, 1.0, 0.0).astype(BF16))
    segment = sums[0:1, :]
    slot = jnp.sum(sums * onehot, axis=0, keepdims=True) - 1.0
    totals = jnp.broadcast_to(jnp.sum(marks, axis=1, keepdims=True), (rows, span))
    owner_chip = owner // 2
    evens = jnp.sum(jnp.where(row_id - 1 == 2 * owner_chip, totals, 0.0), axis=0, keepdims=True)
    own_row = owners_ref[...]
    chip_row = own_row // 2
    odd_row = own_row - 2 * chip_row
    lift = jnp.where(chip_row == my_chip, cap, evens.astype(jnp.int32))
    target = chip_row * (2 * cap) + odd_row * lift + slot.astype(jnp.int32)
    counts[...] = totals[:, 0:HD]
    full = jnp.zeros((1, HD), F32)
    for chip in range(chips):
        pair = counts[2 * chip + 1 : 2 * chip + 2, :] + counts[2 * chip + 2 : 2 * chip + 3, :]
        full = jnp.maximum(full, jnp.where(pair > listed, 1.0, 0.0))
    over[...] = jnp.broadcast_to(full, (KEEP_ROWS, HD))
    lane_row = lax.broadcasted_iota(jnp.int32, (rows, HD), 0)
    mine = jnp.sum(jnp.where(lane_row - 1 == me_h, counts[...], 0.0), axis=0, keepdims=True)
    even = jnp.where(lane_row - 1 == me_h - 1, counts[...], 0.0)
    shift = jnp.sum(even, axis=0, keepdims=True) * my_core.astype(F32)
    info_ref[8:16, :] = jnp.broadcast_to(shift, (8, HD))
    info_ref[16:24, :] = jnp.broadcast_to(mine, (8, HD))
    wide = jnp.broadcast_to(segment, (HD, span)).T
    final = wide[span - 1 : span, :]
    first[...] = jnp.where(wide == 0.0, 1.0, 0.0)
    last[...] = jnp.where(wide == final, 1.0, 0.0)
    keep = jnp.broadcast_to(jnp.where(final == 0.0, 1.0, 0.0), (KEEP_ROWS, HD))
    seg_col[...] = wide
    seg_row[...] = jnp.broadcast_to(segment, (8, span))

    def fill_mask(chunk, carry):
        base = pl.multiple_of(chunk * TILE, TILE)
        same = seg_col[pl.ds(base, TILE), 0:1] == seg_row[0:1, :]
        t_id = base + lax.broadcasted_iota(jnp.int32, (TILE, span), 0)
        s_id = lax.broadcasted_iota(jnp.int32, (TILE, span), 1)
        mask[pl.ds(base, TILE), :] = jnp.where(same & (s_id <= t_id), 1.0, 0.0)
        return carry

    def fill(chunk, carry):
        base = pl.multiple_of(chunk * TILE, TILE)
        place = base + lax.broadcasted_iota(jnp.int32, (TILE, span), 0)
        perm[pl.ds(base, TILE), :] = jnp.where(place == target, 1.0, 0.0).astype(BF16)
        return carry

    def state_copy(step, h):
        return pltpu.make_async_remote_copy(
            src_ref=snd.at[step, h],
            dst_ref=rcv.at[step, h],
            send_sem=st_send.at[step, h],
            recv_sem=st_recv.at[step, h],
            device_id=(partner(step), me_h),
            device_id_type=MESH,
        )

    def state_send(step, h):
        snd[step, h, 0:HD, :] = tot_f[h].astype(BF16)
        snd[step, h, HD : 2 * HD, :] = tot_b[h].astype(BF16)
        snd[step, h, 2 * HD : 2 * HD + KEEP_ROWS, :] = keeps[h, 0].astype(BF16)
        snd[step, h, 2 * HD + KEEP_ROWS :, :] = over[...].astype(BF16)
        state_copy(step, h).start()

    def columns(h):
        return pl.ds(pl.multiple_of(h * HD, HD), HD)

    def local_states(h):
        cols = columns(h)
        k_last = (k_ref[:, cols].astype(F32) * last[...]).astype(BF16)
        q_first = (q_ref[:, cols].astype(F32) * first[...]).astype(BF16)
        tot_f[h] = dot_tn(k_last, v_ref[:, cols])
        tot_b[h] = dot_tn(q_first, o_ref[:, cols])
        in_f[h] = jnp.zeros((HD, HD), F32)
        in_b[h] = jnp.zeros((HD, HD), F32)
        keeps[h, 0] = keep
        keeps[h, 1] = jnp.ones((KEEP_ROWS, HD), F32)
        keeps[h, 2] = jnp.ones((KEEP_ROWS, HD), F32)
        state_send(0, h)

    def combine(step, h):
        state_copy(step, h).wait_recv()
        up = jnp.broadcast_to(upper(step), (HD, HD)) == 1
        up_row = up[0:KEEP_ROWS, :]
        got_f = rcv[step, h, 0:HD, :].astype(F32)
        got_b = rcv[step, h, HD : 2 * HD, :].astype(F32)
        got_keep = rcv[step, h, 2 * HD : 2 * HD + KEEP_ROWS, :].astype(F32)
        over[...] = jnp.maximum(over[...], rcv[step, h, 2 * HD + KEEP_ROWS :, :].astype(F32))
        whole, before, after = keeps[h, 0], keeps[h, 1], keeps[h, 2]
        in_f[h] = in_f[h] + jnp.where(up, before[0:1, :] * got_f, 0.0)
        in_b[h] = in_b[h] + jnp.where(up, 0.0, after[0:1, :] * got_b)
        keeps[h, 1] = jnp.where(up_row, before * got_keep, before)
        keeps[h, 2] = jnp.where(up_row, after, after * got_keep)
        if step < steps - 1:
            mine_f, mine_b = tot_f[h], tot_b[h]
            own, other = whole[0:1, :], got_keep[0:1, :]
            tot_f[h] = jnp.where(up, mine_f + own * got_f, got_f + other * mine_f)
            tot_b[h] = jnp.where(up, got_b + other * mine_b, mine_b + own * got_b)
            keeps[h, 0] = whole * got_keep
            state_send(step + 1, h)

    def near_copy(h):
        return pltpu.make_async_remote_copy(
            src_ref=near_buf.at[h, 1],
            dst_ref=near_ref.at[my_core, :, :, columns(h)],
            send_sem=near_send.at[h],
            recv_sem=near_recv.at[h],
            device_id=(me_s, sibling),
            device_id_type=MESH,
        )

    def own_copy(h):
        return pltpu.make_async_copy(
            near_buf.at[h, 0], near_ref.at[my_core, :, :, columns(h)], own_sem.at[h]
        )

    def far_copy(co, h):
        return pltpu.make_async_remote_copy(
            src_ref=far_buf.at[h, co - 1, :, 0:listed],
            dst_ref=far_ref.at[co - 1, my_core, :, :, columns(h)],
            send_sem=far_send.at[h, co - 1],
            recv_sem=far_recv.at[h, co - 1],
            device_id=(me_s, far_peer(co)),
            device_id_type=MESH,
        )

    def rest_copy(co, h):
        return pltpu.make_async_copy(
            far_buf.at[h, co - 1, :, listed : 2 * cap],
            rest_ref.at[co - 1, :, :, columns(h)],
            rest_sem.at[h, co - 1],
        )

    def pass_on(co, h):
        return pltpu.make_async_remote_copy(
            src_ref=far_ref.at[co - 1, my_core, :, :, columns(h)],
            dst_ref=far_ref.at[co - 1, my_core, :, :, columns(h)],
            send_sem=fwd_send.at[h, co - 1],
            recv_sem=fwd_recv.at[h, co - 1],
            device_id=(me_s, sibling),
            device_id_type=MESH,
        )

    def inner(h):
        cols = columns(h)
        for tile in reversed(range(span // TILE)):
            here = slice(tile * TILE, (tile + 1) * TILE)
            width = (tile + 1) * TILE
            allowed = mask[here, 0:width]
            o_t = o_ref[here, cols]
            q_t = q_ref[here, cols]
            k_s = k_ref[0:width, cols]
            weight = (dot_nt(o_t, v_ref[0:width, cols]) * allowed).astype(BF16)
            acc_q[here, :] = dot_nn(weight, k_s)
            add_k = dot_tn(weight, q_t)
            weight = (dot_nt(q_t, k_s) * allowed).astype(BF16)
            add_v = dot_tn(weight, o_t)
            if width == span:
                acc_k[...] = add_k
                acc_v[...] = add_v
            else:
                acc_k[0:width, :] += add_k
                acc_v[0:width, :] += add_v

    def finish_head(h):
        cols = columns(h)
        fwd = in_f[h].astype(BF16)
        bwd = in_b[h].astype(BF16)
        grad_q = acc_q[...] + first[...] * dot_nt(o_ref[:, cols], fwd)
        grads[:, 0:HD] = grad_q.astype(BF16)
        grad_k = acc_k[...] + last[...] * dot_nt(v_ref[:, cols], bwd)
        grad_v = acc_v[...] + last[...] * dot_nn(k_ref[:, cols], bwd)
        grads[:, HD : 2 * HD] = grad_k.astype(BF16)
        grads[:, 2 * HD :] = grad_v.astype(BF16)
        for co in range(1, chips):
            base = pl.multiple_of(lax.rem(my_chip + co, chips) * (2 * cap), 2 * cap)
            for half in range(2):
                spot = pl.multiple_of(base + half * cap, cap)
                placed = dot_nn(perm[pl.ds(spot, cap), :], grads[...]).astype(BF16)
                for part in range(3):
                    far_buf[h, co - 1, part, half * cap : (half + 1) * cap] = placed[
                        :, part * HD : (part + 1) * HD
                    ]
            far_copy(co, h).start()
            rest_copy(co, h).start()
        for place, peer in ((1, sibling), (0, me_h)):
            base = pl.multiple_of(peer * cap, cap)
            placed = dot_nn(perm[pl.ds(base, cap), :], grads[...]).astype(BF16)
            for part in range(3):
                near_buf[h, place, part] = placed[:, part * HD : (part + 1) * HD]
        near_copy(h).start()
        own_copy(h).start()

    pl.semaphore_wait(barrier, steps + chips)

    def turn(t, carry):
        for lag in range(steps, -1, -1):
            h = t - lag

            @pl.when((h >= 0) & (h < heads))
            def _():
                if lag == 0:
                    local_states(h)
                else:
                    combine(lag - 1, h)
                if lag == steps:
                    finish_head(h)

        @pl.when(t == 0)
        def _():
            lax.fori_loop(0, span // TILE, fill_mask, 0)

        @pl.when(t == 1)
        def _():
            lax.fori_loop(0, n_head * cap // TILE, fill, 0)

        ahead = t - (steps - 1)

        @pl.when((ahead >= 0) & (ahead < heads))
        def _():
            inner(ahead)

        return carry

    lax.fori_loop(0, heads + steps, turn, 0)

    info_ref[0:8, :] = over[0:8, :]

    def forward(h, carry):
        for co in range(1, chips):
            far_copy(co, h).wait_recv()
            pass_on(co, h).start()
        return carry

    lax.fori_loop(0, heads, forward, 0)

    def finish(h, carry):
        for step in range(steps):
            state_copy(step, h).wait_send()
        for co in range(1, chips):
            far_copy(co, h).wait_send()
            rest_copy(co, h).wait()
            pass_on(co, h).wait_send()
            pass_on(co, h).wait_recv()
        near_copy(h).wait_send()
        near_copy(h).wait_recv()
        own_copy(h).wait()
        return carry

    lax.fori_loop(0, heads, finish, 0)


def rest_kernel(n_head, mine_ref, rest_ref, far_send, far_recv, fwd_send, fwd_recv):
    chips = n_head // 2
    me_s = lax.axis_index("seq")
    me_h = lax.axis_index("head")
    my_chip, my_core = lax.div(me_h, 2), lax.rem(me_h, 2)
    sibling = me_h + 1 - 2 * my_core

    def far_peer(co):
        return 2 * lax.rem(my_chip + co, chips) + my_core

    def far_copy(co):
        return pltpu.make_async_remote_copy(
            src_ref=mine_ref.at[co - 1],
            dst_ref=rest_ref.at[co - 1, my_core],
            send_sem=far_send.at[co - 1],
            recv_sem=far_recv.at[co - 1],
            device_id=(me_s, far_peer(co)),
            device_id_type=MESH,
        )

    def pass_on(co):
        return pltpu.make_async_remote_copy(
            src_ref=rest_ref.at[co - 1, my_core],
            dst_ref=rest_ref.at[co - 1, my_core],
            send_sem=fwd_send.at[co - 1],
            recv_sem=fwd_recv.at[co - 1],
            device_id=(me_s, sibling),
            device_id_type=MESH,
        )

    barrier = pltpu.get_barrier_semaphore()
    for peer in [sibling] + [far_peer(co) for co in range(1, chips)]:
        pl.semaphore_signal(barrier, inc=1, device_id=(me_s, peer), device_id_type=MESH)
    pl.semaphore_wait(barrier, chips)
    for co in range(1, chips):
        far_copy(co).start()
    for co in range(1, chips):
        far_copy(co).wait_recv()
        pass_on(co).start()
    for co in range(1, chips):
        far_copy(co).wait_send()
        pass_on(co).wait_send()
        pass_on(co).wait_recv()


def rest_call(n_head, mine):
    lists, parts, rows, feats = mine.shape
    sems = pltpu.SemaphoreType.DMA((lists,))
    return pl.pallas_call(
        functools.partial(rest_kernel, n_head),
        out_shape=jax.ShapeDtypeStruct((lists, 2, parts, rows, feats), BF16),
        in_specs=[pl.BlockSpec(memory_space=pl.ANY)],
        out_specs=pl.BlockSpec(memory_space=pl.ANY),
        scratch_shapes=[sems] * 4,
        compiler_params=pltpu.CompilerParams(collective_id=1, has_side_effects=True),
    )(mine)


def source_of(turn):
    return jnp.where(turn == 1, 2, jnp.where(turn == 2, 1, turn))


def place_kernel(chip_ref, info_ref, near_ref, *refs):
    *lists, out_ref, pick = refs
    cap = out_ref.shape[1]
    source = source_of(pl.program_id(2))

    @pl.when((pl.program_id(0) == 0) & (pl.program_id(1) == 0) & (pl.program_id(2) == 0))
    def _():
        slot = lax.broadcasted_iota(jnp.int32, pick.shape, 0)
        place = lax.broadcasted_iota(jnp.int32, pick.shape, 1)
        shift = info_ref[8:9, 0:1].astype(jnp.int32)
        count = info_ref[16:17, 0:1].astype(jnp.int32)
        pick[...] = jnp.where((place == slot + shift) & (slot < count), 1.0, 0.0).astype(BF16)

    @pl.when(source < 2)
    def _():
        out_ref[...] = near_ref[0]

    @pl.when(source >= 2)
    def _():
        base, total = 0, None
        for ref in lists:
            rows = ref.shape[3]
            term = dot_nn(pick[:, base : base + rows], ref[0, 0, 0])
            total = term if total is None else total + term
            base += rows
        out_ref[0] = total.astype(BF16)


def place_call(n_head, info, near, *lists):
    _, parts, cap, feats = near.shape
    chips = n_head // 2
    wide = 512
    blocks = feats // wide
    chip = lax.div(lax.axis_index("head"), 2).astype(jnp.int32).reshape(1)

    def near_map(part, block, turn, chip_ref):
        return (jnp.where(turn < 2, 0, 1), part, 0, block)

    def list_map(part, block, turn, chip_ref):
        place = jnp.maximum(source_of(turn) - 2, jnp.where(turn == 2, 1, 0))
        return (place // 2, place % 2, part, 0, block)

    def out_map(part, block, turn, chip_ref):
        source = source_of(turn)
        origin = lax.rem(chip_ref[0] + chips - source // 2, chips) * 2 + source % 2
        return (part, 0, origin * blocks + block)

    return pl.pallas_call(
        place_kernel,
        out_shape=jax.ShapeDtypeStruct((parts, cap, n_head * feats), BF16),
        grid_spec=pltpu.PrefetchScalarGridSpec(
            num_scalar_prefetch=1,
            grid=(parts, blocks, n_head),
            in_specs=[
                pl.BlockSpec((24, HD), lambda part, block, turn, chip_ref: (0, 0)),
                pl.BlockSpec((1, 1, cap, wide), near_map),
            ]
            + [pl.BlockSpec((1, 1, 1, a.shape[3], wide), list_map) for a in lists],
            out_specs=pl.BlockSpec((1, cap, wide), out_map),
            scratch_shapes=[pltpu.VMEM((cap, sum(a.shape[3] for a in lists)), BF16)],
        ),
        compiler_params=pltpu.CompilerParams(vmem_limit_bytes=58 * 1024 * 1024),
    )(chip, info, near, *lists)


def shards(n_seq, n_head, queries, keys, values, out_grad, starts, owners):
    span, feats = queries.shape
    heads = feats // HD
    cap = 2 * span // n_head
    steps = n_seq.bit_length() - 1
    vmem = pl.BlockSpec(memory_space=pltpu.VMEM)
    flops = heads * (10 * span * span * HD + 12 * span * span * HD)
    chips = n_head // 2
    listed = list_rows(cap)
    hbm = pl.BlockSpec(memory_space=pl.ANY)
    near, far, rest, info = pl.pallas_call(
        functools.partial(kernel, n_seq, n_head),
        out_shape=[
            jax.ShapeDtypeStruct((2, 3, cap, feats), BF16),
            jax.ShapeDtypeStruct((chips - 1, 2, 3, listed, feats), BF16),
            jax.ShapeDtypeStruct((chips - 1, 3, 2 * cap - listed, feats), BF16),
            jax.ShapeDtypeStruct((24, HD), F32),
        ],
        in_specs=[vmem] * 6,
        out_specs=[hbm, hbm, hbm, vmem],
        scratch_shapes=[
            pltpu.VMEM((span, span), F32),
            pltpu.VMEM((n_head * cap, span), BF16),
            pltpu.VMEM((span, HD), F32),
            pltpu.VMEM((span, HD), F32),
            pltpu.VMEM((heads, HD, HD), F32),
            pltpu.VMEM((heads, HD, HD), F32),
            pltpu.VMEM((heads, HD, HD), F32),
            pltpu.VMEM((heads, HD, HD), F32),
            pltpu.VMEM((heads, 3, KEEP_ROWS, HD), F32),
            pltpu.VMEM((steps, heads, 2 * HD + 2 * KEEP_ROWS, HD), BF16),
            pltpu.VMEM((steps, heads, 2 * HD + 2 * KEEP_ROWS, HD), BF16),
            pltpu.VMEM((span, 3 * HD), BF16),
            pltpu.VMEM((span, HD), F32),
            pltpu.VMEM((span, HD), F32),
            pltpu.VMEM((KEEP_ROWS, HD), F32),
            pltpu.VMEM((16, HD), F32),
            pltpu.VMEM((span, HD), F32),
            pltpu.VMEM((8, span), F32),
            pltpu.VMEM((span, HD), F32),
            pltpu.VMEM((heads, 2, 3, cap, HD), BF16),
            pltpu.VMEM((heads, chips - 1, 3, 2 * cap, HD), BF16),
            pltpu.SemaphoreType.DMA((steps, heads)),
            pltpu.SemaphoreType.DMA((steps, heads)),
            pltpu.SemaphoreType.DMA((heads,)),
            pltpu.SemaphoreType.DMA((heads,)),
            pltpu.SemaphoreType.DMA((heads,)),
            pltpu.SemaphoreType.DMA((heads, chips - 1)),
            pltpu.SemaphoreType.DMA((heads, chips - 1)),
            pltpu.SemaphoreType.DMA((heads, chips - 1)),
            pltpu.SemaphoreType.DMA((heads, chips - 1)),
            pltpu.SemaphoreType.DMA((heads, chips - 1)),
        ],
        compiler_params=pltpu.CompilerParams(
            collective_id=0, has_side_effects=True, vmem_limit_bytes=56 * 1024 * 1024
        ),
        cost_estimate=pl.CostEstimate(
            flops=flops, bytes_accessed=22 * span * feats, transcendentals=0
        ),
    )(queries, keys, values, out_grad, starts.reshape(1, span), owners.reshape(1, span))
    out = lax.cond(
        info[0, 0] > 0.0,
        lambda: place_call(n_head, info, near, far, rest_call(n_head, rest)),
        lambda: place_call(n_head, info, near, far),
    )
    return out.transpose(1, 0, 2)


def solution(mesh):
    in_specs = (
        P("seq", "head"),
        P("seq", "head"),
        P("seq", "head"),
        P("seq", "head"),
        P("seq"),
        P("seq", None),
    )
    return jax.shard_map(
        functools.partial(shards, mesh.shape["seq"], mesh.shape["head"]),
        mesh=mesh,
        in_specs=in_specs,
        out_specs=P(("seq", "head"), None, None),
        check_vma=False,
    )
```

```python
import functools

import jax
import jax.numpy as jnp
from jax import lax
from jax.experimental import pallas as pl
from jax.experimental.pallas import tpu as pltpu
from jax.sharding import PartitionSpec as P

HD = 128
TILE = 256
KEEP_ROWS = 16
LIST_SHARE = (13, 16)
MESH = pl.DeviceIdType.MESH
F32 = jnp.float32
BF16 = jnp.bfloat16


def list_rows(cap):
    return 2 * cap * LIST_SHARE[0] // LIST_SHARE[1] // 16 * 16


def dot_nt(a, b):
    return lax.dot_general(a, b, (((1,), (1,)), ((), ())), preferred_element_type=F32)


def dot_tn(a, b):
    return lax.dot_general(a, b, (((0,), (0,)), ((), ())), preferred_element_type=F32)


def dot_nn(a, b):
    return jnp.dot(a, b, preferred_element_type=F32)


def kernel(
    n_seq,
    n_head,
    q_ref,
    k_ref,
    v_ref,
    o_ref,
    starts_ref,
    owners_ref,
    out_ref,
    rest_ref,
    info_ref,
    mask,
    perm,
    first,
    last,
    tot_f,
    tot_b,
    in_f,
    in_b,
    keeps,
    snd,
    rcv,
    grads,
    acc_k,
    acc_v,
    over,
    counts,
    seg_col,
    seg_row,
    acc_q,
    pick,
    land,
    near_buf,
    far_buf,
    st_send,
    st_recv,
    near_send,
    near_recv,
    own_sem,
    far_send,
    far_recv,
    rest_sem,
    fwd_send,
    fwd_recv,
    put_sem,
):
    span, feats = q_ref.shape
    heads = feats // HD
    cap = 2 * span // n_head
    steps = n_seq.bit_length() - 1
    me_s = lax.axis_index("seq")
    me_h = lax.axis_index("head")
    chips = n_head // 2
    my_chip, my_core = lax.div(me_h, 2), lax.rem(me_h, 2)
    sibling = me_h + 1 - 2 * my_core
    listed = list_rows(cap)

    def upper(step):
        return lax.rem(lax.div(me_s, 1 << step), 2)

    def partner(step):
        return me_s + (1 << step) * (1 - 2 * upper(step))

    def far_peer(co):
        return 2 * lax.rem(my_chip + co, chips) + my_core

    barrier = pltpu.get_barrier_semaphore()
    for step in range(steps):
        pl.semaphore_signal(
            barrier, inc=1, device_id=(partner(step), me_h), device_id_type=MESH
        )
    for peer in [sibling] + [far_peer(co) for co in range(1, chips)]:
        pl.semaphore_signal(barrier, inc=1, device_id=(me_s, peer), device_id_type=MESH)

    rows = 16
    row_id = lax.broadcasted_iota(jnp.int32, (rows, span), 0)
    owner = jnp.broadcast_to(owners_ref[...], (rows, span))
    start = jnp.broadcast_to(starts_ref[...], (rows, span)).astype(F32)
    onehot = jnp.where(row_id - 1 == owner, 1.0, 0.0)
    marks = jnp.where(row_id == 0, start, onehot)
    earlier = lax.broadcasted_iota(jnp.int32, (span, span), 0) <= lax.broadcasted_iota(
        jnp.int32, (span, span), 1
    )
    sums = dot_nn(marks.astype(BF16), jnp.where(earlier, 1.0, 0.0).astype(BF16))
    segment = sums[0:1, :]
    slot = jnp.sum(sums * onehot, axis=0, keepdims=True) - 1.0
    totals = jnp.broadcast_to(jnp.sum(marks, axis=1, keepdims=True), (rows, span))
    owner_chip = owner // 2
    evens = jnp.sum(jnp.where(row_id - 1 == 2 * owner_chip, totals, 0.0), axis=0, keepdims=True)
    own_row = owners_ref[...]
    chip_row = own_row // 2
    odd_row = own_row - 2 * chip_row
    lift = jnp.where(chip_row == my_chip, cap, evens.astype(jnp.int32))
    target = chip_row * (2 * cap) + odd_row * lift + slot.astype(jnp.int32)
    counts[...] = totals[:, 0:HD]
    full = jnp.zeros((1, HD), F32)
    for chip in range(chips):
        pair = counts[2 * chip + 1 : 2 * chip + 2, :] + counts[2 * chip + 2 : 2 * chip + 3, :]
        full = jnp.maximum(full, jnp.where(pair > listed, 1.0, 0.0))
    over[...] = jnp.broadcast_to(full, (KEEP_ROWS, HD))
    lane_row = lax.broadcasted_iota(jnp.int32, (rows, HD), 0)
    mine = jnp.sum(jnp.where(lane_row - 1 == me_h, counts[...], 0.0), axis=0, keepdims=True)
    even = jnp.where(lane_row - 1 == me_h - 1, counts[...], 0.0)
    shift = jnp.sum(even, axis=0, keepdims=True) * my_core.astype(F32)
    info_ref[8:16, :] = jnp.broadcast_to(shift, (8, HD))
    info_ref[16:24, :] = jnp.broadcast_to(mine, (8, HD))
    wide = jnp.broadcast_to(segment, (HD, span)).T
    final = wide[span - 1 : span, :]
    first[...] = jnp.where(wide == 0.0, 1.0, 0.0)
    last[...] = jnp.where(wide == final, 1.0, 0.0)
    keep = jnp.broadcast_to(jnp.where(final == 0.0, 1.0, 0.0), (KEEP_ROWS, HD))
    seg_col[...] = wide
    seg_row[...] = jnp.broadcast_to(segment, (8, span))

    def fill_mask(chunk, carry):
        base = pl.multiple_of(chunk * TILE, TILE)
        same = seg_col[pl.ds(base, TILE), 0:1] == seg_row[0:1, :]
        t_id = base + lax.broadcasted_iota(jnp.int32, (TILE, span), 0)
        s_id = lax.broadcasted_iota(jnp.int32, (TILE, span), 1)
        mask[pl.ds(base, TILE), :] = jnp.where(same & (s_id <= t_id), 1.0, 0.0)
        return carry

    def fill(chunk, carry):
        base = pl.multiple_of(chunk * TILE, TILE)
        place = base + lax.broadcasted_iota(jnp.int32, (TILE, span), 0)
        perm[pl.ds(base, TILE), :] = jnp.where(place == target, 1.0, 0.0).astype(BF16)
        return carry

    def state_copy(step, h):
        return pltpu.make_async_remote_copy(
            src_ref=snd.at[step, h],
            dst_ref=rcv.at[step, h],
            send_sem=st_send.at[step, h],
            recv_sem=st_recv.at[step, h],
            device_id=(partner(step), me_h),
            device_id_type=MESH,
        )

    def state_send(step, h):
        snd[step, h, 0:HD, :] = tot_f[h].astype(BF16)
        snd[step, h, HD : 2 * HD, :] = tot_b[h].astype(BF16)
        snd[step, h, 2 * HD : 2 * HD + KEEP_ROWS, :] = keeps[h, 0].astype(BF16)
        snd[step, h, 2 * HD + KEEP_ROWS :, :] = over[...].astype(BF16)
        state_copy(step, h).start()

    def columns(h):
        return pl.ds(pl.multiple_of(h * HD, HD), HD)

    def local_states(h):
        cols = columns(h)
        k_last = (k_ref[:, cols].astype(F32) * last[...]).astype(BF16)
        q_first = (q_ref[:, cols].astype(F32) * first[...]).astype(BF16)
        tot_f[h] = dot_tn(k_last, v_ref[:, cols])
        tot_b[h] = dot_tn(q_first, o_ref[:, cols])
        in_f[h] = jnp.zeros((HD, HD), F32)
        in_b[h] = jnp.zeros((HD, HD), F32)
        keeps[h, 0] = keep
        keeps[h, 1] = jnp.ones((KEEP_ROWS, HD), F32)
        keeps[h, 2] = jnp.ones((KEEP_ROWS, HD), F32)
        state_send(0, h)

    def combine(step, h):
        state_copy(step, h).wait_recv()
        up = jnp.broadcast_to(upper(step), (HD, HD)) == 1
        up_row = up[0:KEEP_ROWS, :]
        got_f = rcv[step, h, 0:HD, :].astype(F32)
        got_b = rcv[step, h, HD : 2 * HD, :].astype(F32)
        got_keep = rcv[step, h, 2 * HD : 2 * HD + KEEP_ROWS, :].astype(F32)
        over[...] = jnp.maximum(over[...], rcv[step, h, 2 * HD + KEEP_ROWS :, :].astype(F32))
        whole, before, after = keeps[h, 0], keeps[h, 1], keeps[h, 2]
        in_f[h] = in_f[h] + jnp.where(up, before[0:1, :] * got_f, 0.0)
        in_b[h] = in_b[h] + jnp.where(up, 0.0, after[0:1, :] * got_b)
        keeps[h, 1] = jnp.where(up_row, before * got_keep, before)
        keeps[h, 2] = jnp.where(up_row, after, after * got_keep)
        if step < steps - 1:
            mine_f, mine_b = tot_f[h], tot_b[h]
            own, other = whole[0:1, :], got_keep[0:1, :]
            tot_f[h] = jnp.where(up, mine_f + own * got_f, got_f + other * mine_f)
            tot_b[h] = jnp.where(up, got_b + other * mine_b, mine_b + own * got_b)
            keeps[h, 0] = whole * got_keep
            state_send(step + 1, h)

    def out_columns(source, h):
        return pl.ds(pl.multiple_of((source * heads + h) * HD, HD), HD)

    def near_copy(h):
        return pltpu.make_async_remote_copy(
            src_ref=near_buf.at[h, 1],
            dst_ref=out_ref.at[:, :, out_columns(me_h, h)],
            send_sem=near_send.at[h],
            recv_sem=near_recv.at[h],
            device_id=(me_s, sibling),
            device_id_type=MESH,
        )

    def own_copy(h):
        return pltpu.make_async_copy(
            near_buf.at[h, 0], out_ref.at[:, :, out_columns(me_h, h)], own_sem.at[h]
        )

    def far_copy(co, h):
        return pltpu.make_async_remote_copy(
            src_ref=far_buf.at[h, co - 1, :, 0:listed],
            dst_ref=land.at[h, co - 1, my_core],
            send_sem=far_send.at[h, co - 1],
            recv_sem=far_recv.at[h, co - 1],
            device_id=(me_s, far_peer(co)),
            device_id_type=MESH,
        )

    def rest_copy(co, h):
        return pltpu.make_async_copy(
            far_buf.at[h, co - 1, :, listed : 2 * cap],
            rest_ref.at[co - 1, :, :, columns(h)],
            rest_sem.at[h, co - 1],
        )

    def put_copy(co, core, h):
        source = 2 * lax.rem(my_chip + chips - co, chips) + core
        return pltpu.make_async_copy(
            far_buf.at[h, co - 1, :, core * cap : (core + 1) * cap],
            out_ref.at[:, :, out_columns(source, h)],
            put_sem.at[h, co - 1, core],
        )

    def pass_on(co, h):
        return pltpu.make_async_remote_copy(
            src_ref=land.at[h, co - 1, my_core],
            dst_ref=land.at[h, co - 1, my_core],
            send_sem=fwd_send.at[h, co - 1],
            recv_sem=fwd_recv.at[h, co - 1],
            device_id=(me_s, sibling),
            device_id_type=MESH,
        )

    def inner(h):
        cols = columns(h)
        for tile in reversed(range(span // TILE)):
            here = slice(tile * TILE, (tile + 1) * TILE)
            width = (tile + 1) * TILE
            allowed = mask[here, 0:width]
            o_t = o_ref[here, cols]
            q_t = q_ref[here, cols]
            k_s = k_ref[0:width, cols]
            weight = (dot_nt(o_t, v_ref[0:width, cols]) * allowed).astype(BF16)
            acc_q[here, :] = dot_nn(weight, k_s)
            add_k = dot_tn(weight, q_t)
            weight = (dot_nt(q_t, k_s) * allowed).astype(BF16)
            add_v = dot_tn(weight, o_t)
            if width == span:
                acc_k[...] = add_k
                acc_v[...] = add_v
            else:
                acc_k[0:width, :] += add_k
                acc_v[0:width, :] += add_v

    def finish_head(h):
        cols = columns(h)
        fwd = in_f[h].astype(BF16)
        bwd = in_b[h].astype(BF16)
        grad_q = acc_q[...] + first[...] * dot_nt(o_ref[:, cols], fwd)
        grads[:, 0:HD] = grad_q.astype(BF16)
        grad_k = acc_k[...] + last[...] * dot_nt(v_ref[:, cols], bwd)
        grad_v = acc_v[...] + last[...] * dot_nn(k_ref[:, cols], bwd)
        grads[:, HD : 2 * HD] = grad_k.astype(BF16)
        grads[:, 2 * HD :] = grad_v.astype(BF16)
        for co in range(1, chips):
            base = pl.multiple_of(lax.rem(my_chip + co, chips) * (2 * cap), 2 * cap)
            for half in range(2):
                spot = pl.multiple_of(base + half * cap, cap)
                placed = dot_nn(perm[pl.ds(spot, cap), :], grads[...]).astype(BF16)
                for part in range(3):
                    far_buf[h, co - 1, part, half * cap : (half + 1) * cap] = placed[
                        :, part * HD : (part + 1) * HD
                    ]
            far_copy(co, h).start()
            rest_copy(co, h).start()
        for place, peer in ((1, sibling), (0, me_h)):
            base = pl.multiple_of(peer * cap, cap)
            placed = dot_nn(perm[pl.ds(base, cap), :], grads[...]).astype(BF16)
            for part in range(3):
                near_buf[h, place, part] = placed[:, part * HD : (part + 1) * HD]
        near_copy(h).start()
        own_copy(h).start()

    pl.semaphore_wait(barrier, steps + chips)

    def turn(t, carry):
        for lag in range(steps, -1, -1):
            h = t - lag

            @pl.when((h >= 0) & (h < heads))
            def _():
                if lag == 0:
                    local_states(h)
                else:
                    combine(lag - 1, h)
                if lag == steps:
                    finish_head(h)

        @pl.when(t == 0)
        def _():
            lax.fori_loop(0, span // TILE, fill_mask, 0)

        @pl.when(t == 1)
        def _():
            lax.fori_loop(0, n_head * cap // TILE, fill, 0)
            spot = lax.broadcasted_iota(jnp.int32, pick.shape, 0)
            place = lax.broadcasted_iota(jnp.int32, pick.shape, 1)
            moved = info_ref[8:9, 0:1].astype(jnp.int32)
            taken = info_ref[16:17, 0:1].astype(jnp.int32)
            chosen = (place == spot + moved) & (spot < taken)
            pick[...] = jnp.where(chosen, 1.0, 0.0).astype(BF16)

        ahead = t - (steps - 1)

        @pl.when((ahead >= 0) & (ahead < heads))
        def _():
            inner(ahead)

        return carry

    lax.fori_loop(0, heads + steps, turn, 0)

    info_ref[0:8, :] = over[0:8, :]

    def forward(t, carry):
        @pl.when(t < heads)
        def _():
            for co in range(1, chips):
                far_copy(co, t).wait_recv()
                pass_on(co, t).start()

        @pl.when(t > 0)
        def _():
            h = t - 1
            for co in range(1, chips):
                far_copy(co, h).wait_send()
                rest_copy(co, h).wait()
                pass_on(co, h).wait_recv()
                for core in range(2):
                    rows_in = jnp.concatenate(
                        [land[h, co - 1, core, part] for part in range(3)], axis=1
                    )
                    placed = dot_nn(pick[...], rows_in).astype(BF16)
                    for part in range(3):
                        far_buf[h, co - 1, part, core * cap : (core + 1) * cap] = placed[
                            :, part * HD : (part + 1) * HD
                        ]
                    put_copy(co, core, h).start()

        return carry

    lax.fori_loop(0, heads + 1, forward, 0)

    def finish(h, carry):
        for step in range(steps):
            state_copy(step, h).wait_send()
        for co in range(1, chips):
            pass_on(co, h).wait_send()
            for core in range(2):
                put_copy(co, core, h).wait()
        near_copy(h).wait_send()
        near_copy(h).wait_recv()
        own_copy(h).wait()
        return carry

    lax.fori_loop(0, heads, finish, 0)


def rest_kernel(n_head, mine_ref, rest_ref, far_send, far_recv, fwd_send, fwd_recv):
    chips = n_head // 2
    me_s = lax.axis_index("seq")
    me_h = lax.axis_index("head")
    my_chip, my_core = lax.div(me_h, 2), lax.rem(me_h, 2)
    sibling = me_h + 1 - 2 * my_core

    def far_peer(co):
        return 2 * lax.rem(my_chip + co, chips) + my_core

    def far_copy(co):
        return pltpu.make_async_remote_copy(
            src_ref=mine_ref.at[co - 1],
            dst_ref=rest_ref.at[co - 1, my_core],
            send_sem=far_send.at[co - 1],
            recv_sem=far_recv.at[co - 1],
            device_id=(me_s, far_peer(co)),
            device_id_type=MESH,
        )

    def pass_on(co):
        return pltpu.make_async_remote_copy(
            src_ref=rest_ref.at[co - 1, my_core],
            dst_ref=rest_ref.at[co - 1, my_core],
            send_sem=fwd_send.at[co - 1],
            recv_sem=fwd_recv.at[co - 1],
            device_id=(me_s, sibling),
            device_id_type=MESH,
        )

    barrier = pltpu.get_barrier_semaphore()
    for peer in [sibling] + [far_peer(co) for co in range(1, chips)]:
        pl.semaphore_signal(barrier, inc=1, device_id=(me_s, peer), device_id_type=MESH)
    pl.semaphore_wait(barrier, chips)
    for co in range(1, chips):
        far_copy(co).start()
    for co in range(1, chips):
        far_copy(co).wait_recv()
        pass_on(co).start()
    for co in range(1, chips):
        far_copy(co).wait_send()
        pass_on(co).wait_send()
        pass_on(co).wait_recv()


def rest_call(n_head, mine):
    lists, parts, rows, feats = mine.shape
    sems = pltpu.SemaphoreType.DMA((lists,))
    return pl.pallas_call(
        functools.partial(rest_kernel, n_head),
        out_shape=jax.ShapeDtypeStruct((lists, 2, parts, rows, feats), BF16),
        in_specs=[pl.BlockSpec(memory_space=pl.ANY)],
        out_specs=pl.BlockSpec(memory_space=pl.ANY),
        scratch_shapes=[sems] * 4,
        compiler_params=pltpu.CompilerParams(collective_id=1, has_side_effects=True),
    )(mine)


def add_kernel(listed, chip_ref, info_ref, have_ref, rest_ref, out_ref, pick):
    source = pl.program_id(1)

    @pl.when((pl.program_id(0) == 0) & (source == 0))
    def _():
        spot = lax.broadcasted_iota(jnp.int32, pick.shape, 0)
        place = listed + lax.broadcasted_iota(jnp.int32, pick.shape, 1)
        moved = info_ref[8:9, 0:1].astype(jnp.int32)
        taken = info_ref[16:17, 0:1].astype(jnp.int32)
        chosen = (place == spot + moved) & (spot < taken)
        pick[...] = jnp.where(chosen, 1.0, 0.0).astype(BF16)

    @pl.when(source < 2)
    def _():
        out_ref[...] = have_ref[...]

    @pl.when(source >= 2)
    def _():
        more = dot_nn(pick[...], rest_ref[0, 0, 0])
        out_ref[0] = (have_ref[0].astype(F32) + more).astype(BF16)


def add_call(n_head, listed, info, have, rest):
    lists, _, parts, rows, feats = rest.shape
    cap = have.shape[1]
    chips = n_head // 2
    chip = lax.div(lax.axis_index("head"), 2).astype(jnp.int32).reshape(1)

    def rest_map(part, source, chip_ref):
        place = jnp.maximum(source - 2, 0)
        return (place // 2, place % 2, part, 0, 0)

    def out_map(part, source, chip_ref):
        origin = lax.rem(chip_ref[0] + chips - source // 2, chips) * 2 + source % 2
        return (part, 0, origin)

    return pl.pallas_call(
        functools.partial(add_kernel, listed),
        out_shape=jax.ShapeDtypeStruct(have.shape, BF16),
        grid_spec=pltpu.PrefetchScalarGridSpec(
            num_scalar_prefetch=1,
            grid=(parts, n_head),
            in_specs=[
                pl.BlockSpec((24, HD), lambda part, source, chip_ref: (0, 0)),
                pl.BlockSpec((1, cap, feats), out_map),
                pl.BlockSpec((1, 1, 1, rows, feats), rest_map),
            ],
            out_specs=pl.BlockSpec((1, cap, feats), out_map),
            scratch_shapes=[pltpu.VMEM((cap, rows), BF16)],
        ),
        compiler_params=pltpu.CompilerParams(vmem_limit_bytes=58 * 1024 * 1024),
    )(chip, info, have, rest)


def shards(n_seq, n_head, queries, keys, values, out_grad, starts, owners):
    span, feats = queries.shape
    heads = feats // HD
    cap = 2 * span // n_head
    steps = n_seq.bit_length() - 1
    vmem = pl.BlockSpec(memory_space=pltpu.VMEM)
    flops = heads * (10 * span * span * HD + 12 * span * span * HD)
    chips = n_head // 2
    listed = list_rows(cap)
    hbm = pl.BlockSpec(memory_space=pl.ANY)
    out, rest, info = pl.pallas_call(
        functools.partial(kernel, n_seq, n_head),
        out_shape=[
            jax.ShapeDtypeStruct((3, cap, n_head * feats), BF16),
            jax.ShapeDtypeStruct((chips - 1, 3, 2 * cap - listed, feats), BF16),
            jax.ShapeDtypeStruct((24, HD), F32),
        ],
        in_specs=[vmem] * 6,
        out_specs=[hbm, hbm, vmem],
        scratch_shapes=[
            pltpu.VMEM((span, span), F32),
            pltpu.VMEM((n_head * cap, span), BF16),
            pltpu.VMEM((span, HD), F32),
            pltpu.VMEM((span, HD), F32),
            pltpu.VMEM((heads, HD, HD), F32),
            pltpu.VMEM((heads, HD, HD), F32),
            pltpu.VMEM((heads, HD, HD), F32),
            pltpu.VMEM((heads, HD, HD), F32),
            pltpu.VMEM((heads, 3, KEEP_ROWS, HD), F32),
            pltpu.VMEM((steps, heads, 2 * HD + 2 * KEEP_ROWS, HD), BF16),
            pltpu.VMEM((steps, heads, 2 * HD + 2 * KEEP_ROWS, HD), BF16),
            pltpu.VMEM((span, 3 * HD), BF16),
            pltpu.VMEM((span, HD), F32),
            pltpu.VMEM((span, HD), F32),
            pltpu.VMEM((KEEP_ROWS, HD), F32),
            pltpu.VMEM((16, HD), F32),
            pltpu.VMEM((span, HD), F32),
            pltpu.VMEM((8, span), F32),
            pltpu.VMEM((span, HD), F32),
            pltpu.VMEM((cap, listed), BF16),
            pltpu.VMEM((heads, chips - 1, 2, 3, listed, HD), BF16),
            pltpu.VMEM((heads, 2, 3, cap, HD), BF16),
            pltpu.VMEM((heads, chips - 1, 3, 2 * cap, HD), BF16),
            pltpu.SemaphoreType.DMA((steps, heads)),
            pltpu.SemaphoreType.DMA((steps, heads)),
            pltpu.SemaphoreType.DMA((heads,)),
            pltpu.SemaphoreType.DMA((heads,)),
            pltpu.SemaphoreType.DMA((heads,)),
            pltpu.SemaphoreType.DMA((heads, chips - 1)),
            pltpu.SemaphoreType.DMA((heads, chips - 1)),
            pltpu.SemaphoreType.DMA((heads, chips - 1)),
            pltpu.SemaphoreType.DMA((heads, chips - 1)),
            pltpu.SemaphoreType.DMA((heads, chips - 1)),
            pltpu.SemaphoreType.DMA((heads, chips - 1, 2)),
        ],
        compiler_params=pltpu.CompilerParams(
            collective_id=0, has_side_effects=True, vmem_limit_bytes=60 * 1024 * 1024
        ),
        cost_estimate=pl.CostEstimate(
            flops=flops, bytes_accessed=22 * span * feats, transcendentals=0
        ),
    )(queries, keys, values, out_grad, starts.reshape(1, span), owners.reshape(1, span))
    out = lax.cond(
        info[0, 0] > 0.0,
        lambda: add_call(n_head, listed, info, out, rest_call(n_head, rest)),
        lambda: out,
    )
    return out.transpose(1, 0, 2)


def solution(mesh):
    in_specs = (
        P("seq", "head"),
        P("seq", "head"),
        P("seq", "head"),
        P("seq", "head"),
        P("seq"),
        P("seq", None),
    )
    return jax.shard_map(
        functools.partial(shards, mesh.shape["seq"], mesh.shape["head"]),
        mesh=mesh,
        in_specs=in_specs,
        out_specs=P(("seq", "head"), None, None),
        check_vma=False,
    )
```

```python
import functools

import jax
import jax.numpy as jnp
from jax import lax
from jax.experimental import pallas as pl
from jax.experimental.pallas import tpu as pltpu
from jax.sharding import PartitionSpec as P

HD = 128
TILE = 256
KEEP_ROWS = 16
LIST_SHARE = (13, 16)
MESH = pl.DeviceIdType.MESH
F32 = jnp.float32
BF16 = jnp.bfloat16


def list_rows(cap):
    return 2 * cap * LIST_SHARE[0] // LIST_SHARE[1] // 16 * 16


def dot_nt(a, b):
    return lax.dot_general(a, b, (((1,), (1,)), ((), ())), preferred_element_type=F32)


def dot_tn(a, b):
    return lax.dot_general(a, b, (((0,), (0,)), ((), ())), preferred_element_type=F32)


def dot_nn(a, b):
    return jnp.dot(a, b, preferred_element_type=F32)


def kernel(
    n_seq,
    n_head,
    q_hbm,
    k_hbm,
    v_hbm,
    o_hbm,
    starts_ref,
    owners_ref,
    out_ref,
    rest_ref,
    info_ref,
    mask,
    perm,
    first,
    last,
    tot_f,
    tot_b,
    in_f,
    in_b,
    keeps,
    snd,
    rcv,
    grads,
    acc_k,
    acc_v,
    over,
    counts,
    seg_col,
    seg_row,
    acc_q,
    pick,
    land,
    near_buf,
    far_buf,
    st_send,
    st_recv,
    near_send,
    near_recv,
    own_sem,
    far_send,
    far_recv,
    rest_sem,
    fwd_send,
    fwd_recv,
    put_sem,
    q_ref,
    k_ref,
    v_ref,
    o_ref,
    in_sem,
):
    span, feats = q_ref.shape
    heads = feats // HD
    cap = 2 * span // n_head
    steps = n_seq.bit_length() - 1
    me_s = lax.axis_index("seq")
    me_h = lax.axis_index("head")
    chips = n_head // 2
    my_chip, my_core = lax.div(me_h, 2), lax.rem(me_h, 2)
    sibling = me_h + 1 - 2 * my_core
    listed = list_rows(cap)

    def columns(h):
        return pl.ds(pl.multiple_of(h * HD, HD), HD)

    def loads(h):
        pairs = ((q_hbm, q_ref), (k_hbm, k_ref), (v_hbm, v_ref), (o_hbm, o_ref))
        return [
            pltpu.make_async_copy(a.at[:, columns(h)], b.at[:, columns(h)], in_sem.at[i, h])
            for i, (a, b) in enumerate(pairs)
        ]

    def load(h, carry):
        for copy in loads(h):
            copy.start()
        return carry

    lax.fori_loop(0, heads, load, 0)

    def upper(step):
        return lax.rem(lax.div(me_s, 1 << step), 2)

    def partner(step):
        return me_s + (1 << step) * (1 - 2 * upper(step))

    def far_peer(co):
        return 2 * lax.rem(my_chip + co, chips) + my_core

    barrier = pltpu.get_barrier_semaphore()
    for step in range(steps):
        pl.semaphore_signal(
            barrier, inc=1, device_id=(partner(step), me_h), device_id_type=MESH
        )
    for peer in [sibling] + [far_peer(co) for co in range(1, chips)]:
        pl.semaphore_signal(barrier, inc=1, device_id=(me_s, peer), device_id_type=MESH)

    rows = 16
    row_id = lax.broadcasted_iota(jnp.int32, (rows, span), 0)
    owner = jnp.broadcast_to(owners_ref[...], (rows, span))
    start = jnp.broadcast_to(starts_ref[...], (rows, span)).astype(F32)
    onehot = jnp.where(row_id - 1 == owner, 1.0, 0.0)
    marks = jnp.where(row_id == 0, start, onehot)
    earlier = lax.broadcasted_iota(jnp.int32, (span, span), 0) <= lax.broadcasted_iota(
        jnp.int32, (span, span), 1
    )
    sums = dot_nn(marks.astype(BF16), jnp.where(earlier, 1.0, 0.0).astype(BF16))
    segment = sums[0:1, :]
    slot = jnp.sum(sums * onehot, axis=0, keepdims=True) - 1.0
    totals = jnp.broadcast_to(jnp.sum(marks, axis=1, keepdims=True), (rows, span))
    owner_chip = owner // 2
    evens = jnp.sum(jnp.where(row_id - 1 == 2 * owner_chip, totals, 0.0), axis=0, keepdims=True)
    own_row = owners_ref[...]
    chip_row = own_row // 2
    odd_row = own_row - 2 * chip_row
    lift = jnp.where(chip_row == my_chip, cap, evens.astype(jnp.int32))
    target = chip_row * (2 * cap) + odd_row * lift + slot.astype(jnp.int32)
    counts[...] = totals[:, 0:HD]
    full = jnp.zeros((1, HD), F32)
    for chip in range(chips):
        pair = counts[2 * chip + 1 : 2 * chip + 2, :] + counts[2 * chip + 2 : 2 * chip + 3, :]
        full = jnp.maximum(full, jnp.where(pair > listed, 1.0, 0.0))
    over[...] = jnp.broadcast_to(full, (KEEP_ROWS, HD))
    lane_row = lax.broadcasted_iota(jnp.int32, (rows, HD), 0)
    mine = jnp.sum(jnp.where(lane_row - 1 == me_h, counts[...], 0.0), axis=0, keepdims=True)
    even = jnp.where(lane_row - 1 == me_h - 1, counts[...], 0.0)
    shift = jnp.sum(even, axis=0, keepdims=True) * my_core.astype(F32)
    info_ref[8:16, :] = jnp.broadcast_to(shift, (8, HD))
    info_ref[16:24, :] = jnp.broadcast_to(mine, (8, HD))
    wide = jnp.broadcast_to(segment, (HD, span)).T
    final = wide[span - 1 : span, :]
    first[...] = jnp.where(wide == 0.0, 1.0, 0.0)
    last[...] = jnp.where(wide == final, 1.0, 0.0)
    keep = jnp.broadcast_to(jnp.where(final == 0.0, 1.0, 0.0), (KEEP_ROWS, HD))
    seg_col[...] = wide
    seg_row[...] = jnp.broadcast_to(segment, (8, span))

    def fill_mask(chunk, carry):
        base = pl.multiple_of(chunk * TILE, TILE)
        same = seg_col[pl.ds(base, TILE), 0:1] == seg_row[0:1, :]
        t_id = base + lax.broadcasted_iota(jnp.int32, (TILE, span), 0)
        s_id = lax.broadcasted_iota(jnp.int32, (TILE, span), 1)
        mask[pl.ds(base, TILE), :] = jnp.where(same & (s_id <= t_id), 1.0, 0.0)
        return carry

    def fill(chunk, carry):
        base = pl.multiple_of(chunk * TILE, TILE)
        place = base + lax.broadcasted_iota(jnp.int32, (TILE, span), 0)
        perm[pl.ds(base, TILE), :] = jnp.where(place == target, 1.0, 0.0).astype(BF16)
        return carry

    def state_copy(step, h):
        return pltpu.make_async_remote_copy(
            src_ref=snd.at[step, h],
            dst_ref=rcv.at[step, h],
            send_sem=st_send.at[step, h],
            recv_sem=st_recv.at[step, h],
            device_id=(partner(step), me_h),
            device_id_type=MESH,
        )

    def state_send(step, h):
        snd[step, h, 0:HD, :] = tot_f[h].astype(BF16)
        snd[step, h, HD : 2 * HD, :] = tot_b[h].astype(BF16)
        snd[step, h, 2 * HD : 2 * HD + KEEP_ROWS, :] = keeps[h, 0].astype(BF16)
        snd[step, h, 2 * HD + KEEP_ROWS :, :] = over[...].astype(BF16)
        state_copy(step, h).start()

    def local_states(h):
        for copy in loads(h):
            copy.wait()
        cols = columns(h)
        k_last = (k_ref[:, cols].astype(F32) * last[...]).astype(BF16)
        q_first = (q_ref[:, cols].astype(F32) * first[...]).astype(BF16)
        tot_f[h] = dot_tn(k_last, v_ref[:, cols])
        tot_b[h] = dot_tn(q_first, o_ref[:, cols])
        in_f[h] = jnp.zeros((HD, HD), F32)
        in_b[h] = jnp.zeros((HD, HD), F32)
        keeps[h, 0] = keep
        keeps[h, 1] = jnp.ones((KEEP_ROWS, HD), F32)
        keeps[h, 2] = jnp.ones((KEEP_ROWS, HD), F32)
        state_send(0, h)

    def combine(step, h):
        state_copy(step, h).wait_recv()
        up = jnp.broadcast_to(upper(step), (HD, HD)) == 1
        up_row = up[0:KEEP_ROWS, :]
        got_f = rcv[step, h, 0:HD, :].astype(F32)
        got_b = rcv[step, h, HD : 2 * HD, :].astype(F32)
        got_keep = rcv[step, h, 2 * HD : 2 * HD + KEEP_ROWS, :].astype(F32)
        over[...] = jnp.maximum(over[...], rcv[step, h, 2 * HD + KEEP_ROWS :, :].astype(F32))
        whole, before, after = keeps[h, 0], keeps[h, 1], keeps[h, 2]
        in_f[h] = in_f[h] + jnp.where(up, before[0:1, :] * got_f, 0.0)
        in_b[h] = in_b[h] + jnp.where(up, 0.0, after[0:1, :] * got_b)
        keeps[h, 1] = jnp.where(up_row, before * got_keep, before)
        keeps[h, 2] = jnp.where(up_row, after, after * got_keep)
        if step < steps - 1:
            mine_f, mine_b = tot_f[h], tot_b[h]
            own, other = whole[0:1, :], got_keep[0:1, :]
            tot_f[h] = jnp.where(up, mine_f + own * got_f, got_f + other * mine_f)
            tot_b[h] = jnp.where(up, got_b + other * mine_b, mine_b + own * got_b)
            keeps[h, 0] = whole * got_keep
            state_send(step + 1, h)

    def out_columns(source, h):
        return pl.ds(pl.multiple_of((source * heads + h) * HD, HD), HD)

    def near_copy(h):
        return pltpu.make_async_remote_copy(
            src_ref=near_buf.at[h, 1],
            dst_ref=out_ref.at[:, :, out_columns(me_h, h)],
            send_sem=near_send.at[h],
            recv_sem=near_recv.at[h],
            device_id=(me_s, sibling),
            device_id_type=MESH,
        )

    def own_copy(h):
        return pltpu.make_async_copy(
            near_buf.at[h, 0], out_ref.at[:, :, out_columns(me_h, h)], own_sem.at[h]
        )

    def far_copy(co, h):
        return pltpu.make_async_remote_copy(
            src_ref=far_buf.at[h, co - 1, :, 0:listed],
            dst_ref=land.at[h, co - 1, my_core],
            send_sem=far_send.at[h, co - 1],
            recv_sem=far_recv.at[h, co - 1],
            device_id=(me_s, far_peer(co)),
            device_id_type=MESH,
        )

    def rest_copy(co, h):
        return pltpu.make_async_copy(
            far_buf.at[h, co - 1, :, listed : 2 * cap],
            rest_ref.at[co - 1, :, :, columns(h)],
            rest_sem.at[h, co - 1],
        )

    def put_copy(co, core, h):
        source = 2 * lax.rem(my_chip + chips - co, chips) + core
        return pltpu.make_async_copy(
            far_buf.at[h, co - 1, :, core * cap : (core + 1) * cap],
            out_ref.at[:, :, out_columns(source, h)],
            put_sem.at[h, co - 1, core],
        )

    def pass_on(co, h):
        return pltpu.make_async_remote_copy(
            src_ref=land.at[h, co - 1, my_core],
            dst_ref=land.at[h, co - 1, my_core],
            send_sem=fwd_send.at[h, co - 1],
            recv_sem=fwd_recv.at[h, co - 1],
            device_id=(me_s, sibling),
            device_id_type=MESH,
        )

    def inner(h):
        cols = columns(h)
        for tile in reversed(range(span // TILE)):
            here = slice(tile * TILE, (tile + 1) * TILE)
            width = (tile + 1) * TILE
            allowed = mask[here, 0:width]
            o_t = o_ref[here, cols]
            q_t = q_ref[here, cols]
            k_s = k_ref[0:width, cols]
            weight = (dot_nt(o_t, v_ref[0:width, cols]) * allowed).astype(BF16)
            acc_q[here, :] = dot_nn(weight, k_s)
            add_k = dot_tn(weight, q_t)
            weight = (dot_nt(q_t, k_s) * allowed).astype(BF16)
            add_v = dot_tn(weight, o_t)
            if width == span:
                acc_k[...] = add_k
                acc_v[...] = add_v
            else:
                acc_k[0:width, :] += add_k
                acc_v[0:width, :] += add_v

    def finish_head(h):
        cols = columns(h)
        fwd = in_f[h].astype(BF16)
        bwd = in_b[h].astype(BF16)
        grad_q = acc_q[...] + first[...] * dot_nt(o_ref[:, cols], fwd)
        grads[:, 0:HD] = grad_q.astype(BF16)
        grad_k = acc_k[...] + last[...] * dot_nt(v_ref[:, cols], bwd)
        grad_v = acc_v[...] + last[...] * dot_nn(k_ref[:, cols], bwd)
        grads[:, HD : 2 * HD] = grad_k.astype(BF16)
        grads[:, 2 * HD :] = grad_v.astype(BF16)
        for co in range(1, chips):
            base = pl.multiple_of(lax.rem(my_chip + co, chips) * (2 * cap), 2 * cap)
            for half in range(2):
                spot = pl.multiple_of(base + half * cap, cap)
                placed = dot_nn(perm[pl.ds(spot, cap), :], grads[...]).astype(BF16)
                for part in range(3):
                    far_buf[h, co - 1, part, half * cap : (half + 1) * cap] = placed[
                        :, part * HD : (part + 1) * HD
                    ]
            far_copy(co, h).start()
            rest_copy(co, h).start()
        for place, peer in ((1, sibling), (0, me_h)):
            base = pl.multiple_of(peer * cap, cap)
            placed = dot_nn(perm[pl.ds(base, cap), :], grads[...]).astype(BF16)
            for part in range(3):
                near_buf[h, place, part] = placed[:, part * HD : (part + 1) * HD]
        near_copy(h).start()
        own_copy(h).start()

    pl.semaphore_wait(barrier, steps + chips)

    def turn(t, carry):
        for lag in range(steps, -1, -1):
            h = t - lag

            @pl.when((h >= 0) & (h < heads))
            def _():
                if lag == 0:
                    local_states(h)
                else:
                    combine(lag - 1, h)
                if lag == steps:
                    finish_head(h)

        @pl.when(t == 0)
        def _():
            lax.fori_loop(0, span // TILE, fill_mask, 0)

        @pl.when(t == 1)
        def _():
            lax.fori_loop(0, n_head * cap // TILE, fill, 0)
            spot = lax.broadcasted_iota(jnp.int32, pick.shape, 0)
            place = lax.broadcasted_iota(jnp.int32, pick.shape, 1)
            moved = info_ref[8:9, 0:1].astype(jnp.int32)
            taken = info_ref[16:17, 0:1].astype(jnp.int32)
            chosen = (place == spot + moved) & (spot < taken)
            pick[...] = jnp.where(chosen, 1.0, 0.0).astype(BF16)

        ahead = t - (steps - 1)

        @pl.when((ahead >= 0) & (ahead < heads))
        def _():
            inner(ahead)

        return carry

    lax.fori_loop(0, heads + steps, turn, 0)

    info_ref[0:8, :] = over[0:8, :]

    def forward(t, carry):
        @pl.when(t < heads)
        def _():
            for co in range(1, chips):
                far_copy(co, t).wait_recv()
                pass_on(co, t).start()

        @pl.when(t > 0)
        def _():
            h = t - 1
            for co in range(1, chips):
                far_copy(co, h).wait_send()
                rest_copy(co, h).wait()
                pass_on(co, h).wait_recv()
                for core in range(2):
                    rows_in = jnp.concatenate(
                        [land[h, co - 1, core, part] for part in range(3)], axis=1
                    )
                    placed = dot_nn(pick[...], rows_in).astype(BF16)
                    for part in range(3):
                        far_buf[h, co - 1, part, core * cap : (core + 1) * cap] = placed[
                            :, part * HD : (part + 1) * HD
                        ]
                    put_copy(co, core, h).start()

        return carry

    lax.fori_loop(0, heads + 1, forward, 0)

    def finish(h, carry):
        for step in range(steps):
            state_copy(step, h).wait_send()
        for co in range(1, chips):
            pass_on(co, h).wait_send()
            for core in range(2):
                put_copy(co, core, h).wait()
        near_copy(h).wait_send()
        near_copy(h).wait_recv()
        own_copy(h).wait()
        return carry

    lax.fori_loop(0, heads, finish, 0)


def rest_kernel(n_head, mine_ref, rest_ref, far_send, far_recv, fwd_send, fwd_recv):
    chips = n_head // 2
    me_s = lax.axis_index("seq")
    me_h = lax.axis_index("head")
    my_chip, my_core = lax.div(me_h, 2), lax.rem(me_h, 2)
    sibling = me_h + 1 - 2 * my_core

    def far_peer(co):
        return 2 * lax.rem(my_chip + co, chips) + my_core

    def far_copy(co):
        return pltpu.make_async_remote_copy(
            src_ref=mine_ref.at[co - 1],
            dst_ref=rest_ref.at[co - 1, my_core],
            send_sem=far_send.at[co - 1],
            recv_sem=far_recv.at[co - 1],
            device_id=(me_s, far_peer(co)),
            device_id_type=MESH,
        )

    def pass_on(co):
        return pltpu.make_async_remote_copy(
            src_ref=rest_ref.at[co - 1, my_core],
            dst_ref=rest_ref.at[co - 1, my_core],
            send_sem=fwd_send.at[co - 1],
            recv_sem=fwd_recv.at[co - 1],
            device_id=(me_s, sibling),
            device_id_type=MESH,
        )

    barrier = pltpu.get_barrier_semaphore()
    for peer in [sibling] + [far_peer(co) for co in range(1, chips)]:
        pl.semaphore_signal(barrier, inc=1, device_id=(me_s, peer), device_id_type=MESH)
    pl.semaphore_wait(barrier, chips)
    for co in range(1, chips):
        far_copy(co).start()
    for co in range(1, chips):
        far_copy(co).wait_recv()
        pass_on(co).start()
    for co in range(1, chips):
        far_copy(co).wait_send()
        pass_on(co).wait_send()
        pass_on(co).wait_recv()


def rest_call(n_head, mine):
    lists, parts, rows, feats = mine.shape
    sems = pltpu.SemaphoreType.DMA((lists,))
    return pl.pallas_call(
        functools.partial(rest_kernel, n_head),
        out_shape=jax.ShapeDtypeStruct((lists, 2, parts, rows, feats), BF16),
        in_specs=[pl.BlockSpec(memory_space=pl.ANY)],
        out_specs=pl.BlockSpec(memory_space=pl.ANY),
        scratch_shapes=[sems] * 4,
        compiler_params=pltpu.CompilerParams(collective_id=1, has_side_effects=True),
    )(mine)


def add_kernel(listed, chip_ref, info_ref, have_ref, rest_ref, out_ref, pick):
    source = pl.program_id(1)

    @pl.when((pl.program_id(0) == 0) & (source == 0))
    def _():
        spot = lax.broadcasted_iota(jnp.int32, pick.shape, 0)
        place = listed + lax.broadcasted_iota(jnp.int32, pick.shape, 1)
        moved = info_ref[8:9, 0:1].astype(jnp.int32)
        taken = info_ref[16:17, 0:1].astype(jnp.int32)
        chosen = (place == spot + moved) & (spot < taken)
        pick[...] = jnp.where(chosen, 1.0, 0.0).astype(BF16)

    @pl.when(source < 2)
    def _():
        out_ref[...] = have_ref[...]

    @pl.when(source >= 2)
    def _():
        more = dot_nn(pick[...], rest_ref[0, 0, 0])
        out_ref[0] = (have_ref[0].astype(F32) + more).astype(BF16)


def add_call(n_head, listed, info, have, rest):
    lists, _, parts, rows, feats = rest.shape
    cap = have.shape[1]
    chips = n_head // 2
    chip = lax.div(lax.axis_index("head"), 2).astype(jnp.int32).reshape(1)

    def rest_map(part, source, chip_ref):
        place = jnp.maximum(source - 2, 0)
        return (place // 2, place % 2, part, 0, 0)

    def out_map(part, source, chip_ref):
        origin = lax.rem(chip_ref[0] + chips - source // 2, chips) * 2 + source % 2
        return (part, 0, origin)

    return pl.pallas_call(
        functools.partial(add_kernel, listed),
        out_shape=jax.ShapeDtypeStruct(have.shape, BF16),
        grid_spec=pltpu.PrefetchScalarGridSpec(
            num_scalar_prefetch=1,
            grid=(parts, n_head),
            in_specs=[
                pl.BlockSpec((24, HD), lambda part, source, chip_ref: (0, 0)),
                pl.BlockSpec((1, cap, feats), out_map),
                pl.BlockSpec((1, 1, 1, rows, feats), rest_map),
            ],
            out_specs=pl.BlockSpec((1, cap, feats), out_map),
            scratch_shapes=[pltpu.VMEM((cap, rows), BF16)],
        ),
        compiler_params=pltpu.CompilerParams(vmem_limit_bytes=58 * 1024 * 1024),
    )(chip, info, have, rest)


def shards(n_seq, n_head, queries, keys, values, out_grad, starts, owners):
    span, feats = queries.shape
    heads = feats // HD
    cap = 2 * span // n_head
    steps = n_seq.bit_length() - 1
    vmem = pl.BlockSpec(memory_space=pltpu.VMEM)
    flops = heads * (10 * span * span * HD + 12 * span * span * HD)
    chips = n_head // 2
    listed = list_rows(cap)
    hbm = pl.BlockSpec(memory_space=pl.ANY)
    out, rest, info = pl.pallas_call(
        functools.partial(kernel, n_seq, n_head),
        out_shape=[
            jax.ShapeDtypeStruct((3, cap, n_head * feats), BF16),
            jax.ShapeDtypeStruct((chips - 1, 3, 2 * cap - listed, feats), BF16),
            jax.ShapeDtypeStruct((24, HD), F32),
        ],
        in_specs=[hbm] * 4 + [vmem] * 2,
        out_specs=[hbm, hbm, vmem],
        scratch_shapes=[
            pltpu.VMEM((span, span), F32),
            pltpu.VMEM((n_head * cap, span), BF16),
            pltpu.VMEM((span, HD), F32),
            pltpu.VMEM((span, HD), F32),
            pltpu.VMEM((heads, HD, HD), F32),
            pltpu.VMEM((heads, HD, HD), F32),
            pltpu.VMEM((heads, HD, HD), F32),
            pltpu.VMEM((heads, HD, HD), F32),
            pltpu.VMEM((heads, 3, KEEP_ROWS, HD), F32),
            pltpu.VMEM((steps, heads, 2 * HD + 2 * KEEP_ROWS, HD), BF16),
            pltpu.VMEM((steps, heads, 2 * HD + 2 * KEEP_ROWS, HD), BF16),
            pltpu.VMEM((span, 3 * HD), BF16),
            pltpu.VMEM((span, HD), F32),
            pltpu.VMEM((span, HD), F32),
            pltpu.VMEM((KEEP_ROWS, HD), F32),
            pltpu.VMEM((16, HD), F32),
            pltpu.VMEM((span, HD), F32),
            pltpu.VMEM((8, span), F32),
            pltpu.VMEM((span, HD), F32),
            pltpu.VMEM((cap, listed), BF16),
            pltpu.VMEM((heads, chips - 1, 2, 3, listed, HD), BF16),
            pltpu.VMEM((heads, 2, 3, cap, HD), BF16),
            pltpu.VMEM((heads, chips - 1, 3, 2 * cap, HD), BF16),
            pltpu.SemaphoreType.DMA((steps, heads)),
            pltpu.SemaphoreType.DMA((steps, heads)),
            pltpu.SemaphoreType.DMA((heads,)),
            pltpu.SemaphoreType.DMA((heads,)),
            pltpu.SemaphoreType.DMA((heads,)),
            pltpu.SemaphoreType.DMA((heads, chips - 1)),
            pltpu.SemaphoreType.DMA((heads, chips - 1)),
            pltpu.SemaphoreType.DMA((heads, chips - 1)),
            pltpu.SemaphoreType.DMA((heads, chips - 1)),
            pltpu.SemaphoreType.DMA((heads, chips - 1)),
            pltpu.SemaphoreType.DMA((heads, chips - 1, 2)),
            pltpu.VMEM((span, feats), BF16),
            pltpu.VMEM((span, feats), BF16),
            pltpu.VMEM((span, feats), BF16),
            pltpu.VMEM((span, feats), BF16),
            pltpu.SemaphoreType.DMA((4, heads)),
        ],
        compiler_params=pltpu.CompilerParams(
            collective_id=0, has_side_effects=True, vmem_limit_bytes=60 * 1024 * 1024
        ),
        cost_estimate=pl.CostEstimate(
            flops=flops, bytes_accessed=22 * span * feats, transcendentals=0
        ),
    )(queries, keys, values, out_grad, starts.reshape(1, span), owners.reshape(1, span))
    out = lax.cond(
        info[0, 0] > 0.0,
        lambda: add_call(n_head, listed, info, out, rest_call(n_head, rest)),
        lambda: out,
    )
    return out.transpose(1, 0, 2)


def solution(mesh):
    in_specs = (
        P("seq", "head"),
        P("seq", "head"),
        P("seq", "head"),
        P("seq", "head"),
        P("seq"),
        P("seq", None),
    )
    return jax.shard_map(
        functools.partial(shards, mesh.shape["seq"], mesh.shape["head"]),
        mesh=mesh,
        in_specs=in_specs,
        out_specs=P(("seq", "head"), None, None),
        check_vma=False,
    )
```
